128 devices in a mesh: row: 32 (over y, x, core), col: 4 (over z).
Axes of the slice: x: 4, y: 4, z: 4, core: 2. Of those that a mesh axis runs over, the one named last changes fastest.
Arguments:
- node_query: bfloat16 [16384, 1024], P(('row', 'col')), may hold values from -400 to 400
- node_key: bfloat16 [16384, 1024], P(('col', 'row')), may hold values from -9 to 9
- node_value: bfloat16 [16384, 1024], P(('col', 'row')), may hold values from -8 to 8
- grad_out: bfloat16 [16384, 1024], P(('row', 'col')), may hold values from -8 to 8
- block_adjacency: int32 [128, 128], P('row', 'col'), may hold values from 0 to 1, as said below
- edge_mask: int32 [16384, 16384], P('row', 'col'), may hold values from 0 to 1
Outputs:
- attended: bfloat16 [16384, 1024], P(('row', 'col'))
- grad_query: bfloat16 [16384, 1024], P(('row', 'col'))
- grad_key: bfloat16 [16384, 1024], P(('col', 'row'))
- grad_value: bfloat16 [16384, 1024], P(('col', 'row'))
The draws below stay inside these ranges and needn't reach their ends.
Inputs may be any that keep to these rules, and one draw needn't show every extreme that they name: `block_adjacency`: among the 4 target blocks of one index of row and the 32 source blocks of one index of col, between 4 and 32 tiles are 1, and exactly 32 for some such pair; every target block has a tile of 1 in which each of its target nodes has an edge in edge_mask.
All inputs are finite; a program needn't handle non-finite values.
Results may differ from the reference program's by a relative error of at most 0.024.
Values may be sent and summed in bfloat16 or wider, within the bound.
No kernel may reach another device: no remote copies, remote signals or barrier semaphores. Data moves between devices by JAX's collectives and lax.ppermute only.
A program may use at most 256 MiB of HBM per device.

```python
import math
import jax
import jax.numpy as jnp
from jax import lax

D = 1024
HEADS = 16
BLK = 128
TB = 4
SB = 32
MAXT = 32
NTB = 128
NSB = 128
NT = 16384
NS = 16384
N_ROW = 32
N_COL = 4


def forced_tiles(key):
    chosen = jax.random.randint(jax.random.fold_in(key, 11), (NTB,), 0, NSB)
    offset = 2 * jax.random.randint(jax.random.fold_in(key, 12), (NT,), 0, BLK // 2)
    first_col = chosen[jnp.arange(NT) // BLK] * BLK + offset
    return (chosen, first_col)


def key_table(key):
    drawn = jnp.clip(jax.random.normal(jax.random.fold_in(key, 21), (NS, D), jnp.float32), -6.0, 6.0)
    return drawn


def draw_node_key(key, part):
    key_rows = key_table(key)
    return key_rows.astype(jnp.bfloat16)


def draw_node_query(key, part):
    result = jnp.clip(jax.random.normal(jax.random.fold_in(key, 31), (NT, D), jnp.float32), -6.0, 6.0)
    return result.astype(jnp.bfloat16)


def draw_block_adjacency(key, part):
    chosen, first_col = forced_tiles(key)
    per_block = TB * SB
    forced = jnp.arange(NSB)[None, :] == chosen[:, None]
    forced_grid = forced.reshape(N_ROW, TB, N_COL, SB).transpose(0, 2, 1, 3).reshape(N_ROW, N_COL, per_block)
    jitter = jax.random.randint(jax.random.fold_in(key, 13), (N_ROW, N_COL, per_block), 1, 65536)
    places = jnp.arange(per_block)
    scores = jnp.where(forced_grid, 0, jitter) * per_block + places
    rank_of = jnp.sum((scores[..., None, :] < scores[..., :, None]).astype(jnp.int32), axis=-1)
    base_count = TB + jax.random.randint(jax.random.fold_in(key, 14), (N_ROW, N_COL), 0, (MAXT - TB) // 2 + 1)
    heavy_block = jax.random.randint(jax.random.fold_in(key, 15), (N_ROW, N_COL), 0, 8) == 0
    pick_row = jax.random.randint(jax.random.fold_in(key, 16), (), 0, N_ROW)
    pick_col = jax.random.randint(jax.random.fold_in(key, 17), (), 0, N_COL)
    target = jnp.where(heavy_block, MAXT, base_count)
    picked = (jnp.arange(N_ROW)[:, None] == pick_row) & (jnp.arange(N_COL)[None, :] == pick_col)
    target = jnp.where(picked, MAXT, target)
    chosen_tiles = (rank_of < target[..., None]).astype(jnp.int32)
    return chosen_tiles.reshape(N_ROW, N_COL, TB, SB).transpose(0, 2, 1, 3).reshape(NTB, NSB)


def draw_edge_mask(key, part):
    chosen, first_col = forced_tiles(key)
    columns = jnp.arange(NS)[None, :]
    random_edge = jax.random.randint(jax.random.fold_in(key, 18), (NT, NS), 0, 64) == 0
    forced_edge = (columns == first_col[:, None]) | (columns == first_col[:, None] + 1)
    return (random_edge | forced_edge).astype(jnp.int32)


def shard_levels(rng, extent, shards, least, largest):
    def one(dim, parts):
        draws = jax.random.uniform(jax.random.fold_in(jax.random.fold_in(rng, 6), dim), (parts,), jnp.float32, least / len(shards), largest / len(shards))
        return jnp.repeat(jnp.exp(draws), extent[dim] // parts).reshape((-1,) + (1,) * (len(extent) - dim - 1))

    gain = one(*shards[0])
    for cut in shards[1:]:
        gain = gain * one(*cut)
    return gain


def centred(own_key, extent, deviation, most, pieces=(), kind=jnp.bfloat16):
    drawn = jax.random.normal(own_key, extent, jnp.float32) * deviation
    if len(pieces) > 0:
        drawn = shard_levels(own_key, extent, pieces, -0.22, 0.18) * drawn
    return jnp.clip(drawn, min=-most, max=most).astype(kind)


def setup_inputs(seed: int = 0) -> dict:
    seeds = jax.random.split(jax.random.key(seed), 7)
    return {
        "node_query": draw_node_query(jax.random.fold_in(seeds[6], 71), 0),
        "node_key": draw_node_key(jax.random.fold_in(seeds[6], 71), 0),
        "node_value": centred(seeds[2], (NS, D), 2.0, 8.0, ((0, 128),)),
        "grad_out": centred(seeds[3], (NT, D), 2.0, 8.0, ((0, 128),)),
        "block_adjacency": draw_block_adjacency(jax.random.fold_in(seeds[6], 71), 0),
        "edge_mask": draw_edge_mask(jax.random.fold_in(seeds[6], 71), 0),
    }


very_low = -1e+30

def reference(node_query, node_key, node_value, grad_out, block_adjacency, edge_mask):
    head_dim = D // HEADS
    score_scale = 1.0 / math.sqrt(head_dim)
    key_heads = node_key.astype(jnp.float32).reshape(NS, HEADS, head_dim)
    value_heads = node_value.astype(jnp.float32).reshape(NS, HEADS, head_dim)
    query_blocks = node_query.astype(jnp.float32).reshape(NTB, BLK, HEADS, head_dim)
    grad_blocks = grad_out.astype(jnp.float32).reshape(NTB, BLK, HEADS, head_dim)
    mask_blocks = edge_mask.reshape(NTB, BLK, NS)
    adjacency_cols = jnp.repeat(block_adjacency, BLK, axis=1)

    def block_step(carried, inputs):
        key_sum, value_sum = carried
        query_block, grad_block, mask_block, adjacency_row = inputs
        allowed = (mask_block * adjacency_row[None, :] > 0)[:, None, :]
        scores = jnp.einsum('qhe,khe->qhk', query_block, key_heads) * score_scale
        row_max = lax.optimization_barrier(jnp.max(jnp.where(allowed, scores, very_low), axis=-1))
        exponent = jnp.where(allowed, jnp.exp(scores - row_max[..., None]), 0.0)
        row_total = lax.optimization_barrier(jnp.sum(exponent, axis=-1))
        weights = lax.optimization_barrier(exponent.astype(jnp.bfloat16)).astype(jnp.float32)
        summed = jnp.einsum('qhk,khe->qhe', weights, value_heads)
        attended = (summed / row_total[..., None]).astype(jnp.bfloat16)
        attended_wide = lax.optimization_barrier(attended).astype(jnp.float32)
        log_total = row_max + jnp.log(row_total)
        row_delta = lax.optimization_barrier(jnp.sum(grad_block * attended_wide, axis=-1))
        probs = jnp.where(allowed, jnp.exp(scores - log_total[..., None]), 0.0)
        probs_low = lax.optimization_barrier(probs.astype(jnp.bfloat16)).astype(jnp.float32)
        value_part = jnp.einsum('qhk,qhe->khe', probs_low, grad_block)
        grad_prob = jnp.einsum('qhe,khe->qhk', grad_block, value_heads)
        grad_score = (probs * (grad_prob - row_delta[..., None]) * score_scale).astype(jnp.bfloat16)
        grad_score = lax.optimization_barrier(grad_score).astype(jnp.float32)
        query_part = jnp.einsum('qhk,khe->qhe', grad_score, key_heads).astype(jnp.bfloat16)
        key_part = jnp.einsum('qhk,qhe->khe', grad_score, query_block)
        return ((key_sum + key_part, value_sum + value_part), (attended, query_part))
    start = (jnp.zeros((NS, HEADS, head_dim), jnp.float32), jnp.zeros((NS, HEADS, head_dim), jnp.float32))
    (key_sum, value_sum), (attended, query_grad) = lax.scan(block_step, start, (query_blocks, grad_blocks, mask_blocks, adjacency_cols))
    attended = attended.reshape(NT, D)
    grad_query = query_grad.reshape(NT, D)
    grad_key = key_sum.reshape(NS, D).astype(jnp.bfloat16)
    grad_value = value_sum.reshape(NS, D).astype(jnp.bfloat16)
    return (attended, grad_query, grad_key, grad_value)
```

```python
import functools
import math

import jax
import jax.numpy as jnp
from jax import lax
from jax.experimental import pallas as pl
from jax.experimental.pallas import tpu as pltpu
from jax.sharding import Mesh
from jax.sharding import PartitionSpec as P

D = 1024
HEADS = 16
BLK = 128
HEAD = D // HEADS
PAIRS = HEADS // 2
NT = 8
NS = 16
PP = 2
W = PP * BLK
LOW = -1e30
BASE2 = math.log2(math.e) / math.sqrt(HEAD)
SCALE = 1.0 / math.sqrt(HEAD)
f32 = jnp.float32
bf16 = jnp.bfloat16
VMEM = 56 * 1024 * 1024
EMPTY = 2 * 4 * NS

nt_dims = (((1,), (1,)), ((), ()))


def dot_nt(a, b):
    return lax.dot_general(a, b, nt_dims, preferred_element_type=f32)


def dot(a, b):
    return jnp.dot(a, b, preferred_element_type=f32)


def split_pair(tile):
    lane = lax.broadcasted_iota(jnp.int32, tile.shape, 1)
    zero = jnp.zeros_like(tile)
    return jnp.concatenate(
        [jnp.where(lane < HEAD, tile, zero), jnp.where(lane >= HEAD, tile, zero)], axis=0
    )


def bias_kernel(side, mask_ref, own_ref, send_ref):
    even = side[0] == 0
    for j in range(NS):
        tiles = []
        for par in range(2):
            start = (2 * j + par) * BLK
            edge = mask_ref[:, start : start + BLK]
            tiles.append(jnp.where(edge > 0, 0.0, LOW).astype(f32).T)
        first = jnp.where(even, tiles[0], tiles[1])
        second = jnp.where(even, tiles[1], tiles[0])
        own_ref[j] = first.astype(bf16)
        send_ref[j] = second.astype(bf16)


def bias_tiles(side, edge_mask):
    shape = jax.ShapeDtypeStruct((4 * NS, BLK, BLK), bf16)
    spec = pl.BlockSpec((NS, BLK, BLK), lambda i, s: (i, 0, 0))
    return pl.pallas_call(
        bias_kernel,
        grid_spec=pltpu.PrefetchScalarGridSpec(
            num_scalar_prefetch=1,
            grid=(4,),
            in_specs=[pl.BlockSpec((BLK, 2 * NS * BLK), lambda i, s: (i, 0))],
            out_specs=[spec, spec],
        ),
        out_shape=[shape, shape],
        compiler_params=pltpu.CompilerParams(vmem_limit_bytes=VMEM),
        cost_estimate=pl.CostEstimate(flops=0, bytes_accessed=30 * 2**20, transcendentals=0),
        name="bias_tiles",
    )(side, edge_mask)


def slots(meta, lt, i):
    at = NT + lt * NS + 2 * i
    return meta[at], meta[at + 1], meta[at + NT * NS], meta[at + NT * NS + 1]


def cols(pp):
    return slice(pp * BLK, (pp + 1) * BLK)


def heads_wide(first, second):
    return jnp.concatenate([first, second], axis=1)


def head_rows(pair):
    return jnp.concatenate([pair[:, :BLK], pair[:, BLK:]], axis=0)


def forward_kernel(meta, qg_ref, kv_ref, bias_ref, acc_ref, stat_ref, vt_ref):
    def turn(sb, _):
        for pp in range(PP):
            vt_ref[sb, cols(pp), :] = kv_ref[sb, 1, :, cols(pp)].T
        return 0

    lax.fori_loop(0, NS, turn, 0)

    def target(lt, _):
        queries = [split_pair(qg_ref[lt, 0, :, cols(pp)]) for pp in range(PP)]

        def step(i, state):
            s0, s1, b0, b1 = slots(meta, lt, i)
            bias = jnp.concatenate([bias_ref[b0], bias_ref[b1]], axis=0).astype(f32)
            bias = heads_wide(bias, bias)
            out = []
            for pp in range(PP):
                top, total, acc = state[pp]
                keys = jnp.concatenate(
                    [kv_ref[s0, 0, :, cols(pp)], kv_ref[s1, 0, :, cols(pp)]], axis=0
                )
                scores = dot_nt(keys, queries[pp]) * BASE2 + bias
                new_top = jnp.maximum(top, jnp.max(scores, axis=0, keepdims=True))
                factor = jnp.exp2(top - new_top)
                weights = jnp.exp2(scores - new_top)
                total = total * factor + jnp.sum(weights, axis=0, keepdims=True)
                low = weights.astype(bf16)
                vt = heads_wide(vt_ref[s0, cols(pp), :], vt_ref[s1, cols(pp), :])
                part = heads_wide(
                    dot(vt[:HEAD], low[:, :BLK]), dot(vt[HEAD:], low[:, BLK:])
                )
                out.append((new_top, total, acc * factor + part))
            return tuple(out)

        start = tuple(
            (
                jnp.full((1, 2 * BLK), LOW, f32),
                jnp.zeros((1, 2 * BLK), f32),
                jnp.zeros((HEAD, 2 * BLK), f32),
            )
            for _ in range(PP)
        )
        state = lax.fori_loop(0, (meta[lt] + 1) // 2, step, start)
        for pp in range(PP):
            top, total, acc = state[pp]
            grad = qg_ref[lt, 1, :, cols(pp)].astype(f32).T
            grad = heads_wide(grad[:HEAD], grad[HEAD:])
            acc_ref[lt, pp] = acc
            stat_ref[pp, pl.ds(lt, 1), :] = top
            stat_ref[pp, pl.ds(NT + lt, 1), :] = total
            stat_ref[pp, pl.ds(2 * NT + lt, 1), :] = jnp.sum(acc * grad, axis=0, keepdims=True)
        return 0

    lax.fori_loop(0, NT, target, 0)


def forward(meta, qg, kv, bias):
    groups = qg.shape[-1] // W
    return pl.pallas_call(
        forward_kernel,
        grid_spec=pltpu.PrefetchScalarGridSpec(
            num_scalar_prefetch=1,
            grid=(groups,),
            in_specs=[
                pl.BlockSpec((NT, 2, BLK, W), lambda p, s: (0, 0, 0, p)),
                pl.BlockSpec((NS, 2, BLK, W), lambda p, s: (0, 0, 0, p)),
                pl.BlockSpec((EMPTY + 1, BLK, BLK), lambda p, s: (0, 0, 0)),
            ],
            out_specs=[
                pl.BlockSpec((NT, PP, HEAD, 2 * BLK), lambda p, s: (0, p, 0, 0)),
                pl.BlockSpec((PP, 3 * NT, 2 * BLK), lambda p, s: (p, 0, 0)),
            ],
            scratch_shapes=[pltpu.VMEM((NS, W, BLK), bf16)],
        ),
        out_shape=[
            jax.ShapeDtypeStruct((NT, groups * PP, HEAD, 2 * BLK), f32),
            jax.ShapeDtypeStruct((groups * PP, 3 * NT, 2 * BLK), f32),
        ],
        compiler_params=pltpu.CompilerParams(vmem_limit_bytes=VMEM),
        cost_estimate=pl.CostEstimate(
            flops=10**10, bytes_accessed=20 * 2**20, transcendentals=10**7
        ),
        name="forward",
    )(meta, qg, kv, bias)


def backward_kernel(
    meta, qg_ref, kv_ref, bias_ref, acc_ref, own_ref, all_ref, dkv_ref, dqa_ref, kt_ref, sum_ref, row_ref
):
    def turn(sb, _):
        for pp in range(PP):
            kt_ref[sb, cols(pp), :] = kv_ref[sb, 0, :, cols(pp)].T
        return 0

    lax.fori_loop(0, NS, turn, 0)
    sum_ref[...] = jnp.zeros_like(sum_ref)
    for pp in range(PP):
        tops = all_ref[:, pp, :NT, :]
        top = jnp.max(tops, axis=0)
        factors = jnp.exp2(tops - top[None])
        total = jnp.sum(all_ref[:, pp, NT : 2 * NT, :] * factors, axis=0)
        delta = jnp.sum(all_ref[:, pp, 2 * NT :, :] * factors, axis=0)
        log_total = top + jnp.log2(total)
        row_ref[pp, :NT, :] = log_total
        row_ref[pp, NT : 2 * NT, :] = delta / total
        row_ref[pp, 2 * NT :, :] = jnp.exp2(own_ref[pp, :NT, :] - log_total)

    def target(lt, _):
        queries = [split_pair(qg_ref[lt, 0, :, cols(pp)]) for pp in range(PP)]
        grads = [split_pair(qg_ref[lt, 1, :, cols(pp)]) for pp in range(PP)]
        log_totals = [row_ref[pp, pl.ds(lt, 1), :] for pp in range(PP)]
        deltas = [row_ref[pp, pl.ds(NT + lt, 1), :] for pp in range(PP)]

        def step(i, state):
            s0, s1, b0, b1 = slots(meta, lt, i)
            bias = jnp.concatenate([bias_ref[b0], bias_ref[b1]], axis=0).astype(f32)
            bias = heads_wide(bias, bias)
            out = []
            for pp in range(PP):
                keys = jnp.concatenate(
                    [kv_ref[s0, 0, :, cols(pp)], kv_ref[s1, 0, :, cols(pp)]], axis=0
                )
                values = jnp.concatenate(
                    [kv_ref[s0, 1, :, cols(pp)], kv_ref[s1, 1, :, cols(pp)]], axis=0
                )
                scores = dot_nt(keys, queries[pp]) * BASE2 + bias
                probs = jnp.exp2(scores - log_totals[pp])
                grad_prob = dot_nt(values, grads[pp])
                grad_score = (probs * (grad_prob - deltas[pp])).astype(bf16)
                value_part = dot(probs.astype(bf16), grads[pp])
                key_part = dot(grad_score, queries[pp])
                sum_ref[s0, 0, :, cols(pp)] += key_part[:BLK]
                sum_ref[s1, 0, :, cols(pp)] += key_part[BLK:]
                sum_ref[s0, 1, :, cols(pp)] += value_part[:BLK]
                sum_ref[s1, 1, :, cols(pp)] += value_part[BLK:]
                kt = heads_wide(kt_ref[s0, cols(pp), :], kt_ref[s1, cols(pp), :])
                part = heads_wide(
                    dot(kt[:HEAD], grad_score[:, :BLK]), dot(kt[HEAD:], grad_score[:, BLK:])
                )
                out.append(state[pp] + part)
            return tuple(out)

        start = tuple(jnp.zeros((HEAD, 2 * BLK), f32) for _ in range(PP))
        state = lax.fori_loop(0, (meta[lt] + 1) // 2, step, start)
        for pp in range(PP):
            attended = acc_ref[lt, pp] * row_ref[pp, pl.ds(2 * NT + lt, 1), :]
            dqa_ref[lt, 0, :, cols(pp)] = head_rows(attended).T.astype(bf16)
            dqa_ref[lt, 1, :, cols(pp)] = (head_rows(state[pp]).T * SCALE).astype(bf16)
        return 0

    lax.fori_loop(0, NT, target, 0)
    dkv_ref[:, 0] = (sum_ref[:, 0] * SCALE).astype(bf16)
    dkv_ref[:, 1] = sum_ref[:, 1].astype(bf16)


def backward(meta, qg, kv, bias, acc, own, stats):
    groups = qg.shape[-1] // W
    width = groups * W
    n = stats.shape[0]
    return pl.pallas_call(
        backward_kernel,
        grid_spec=pltpu.PrefetchScalarGridSpec(
            num_scalar_prefetch=1,
            grid=(groups,),
            in_specs=[
                pl.BlockSpec((NT, 2, BLK, W), lambda p, s: (0, 0, 0, p)),
                pl.BlockSpec((NS, 2, BLK, W), lambda p, s: (0, 0, 0, p)),
                pl.BlockSpec((EMPTY + 1, BLK, BLK), lambda p, s: (0, 0, 0)),
                pl.BlockSpec((NT, PP, HEAD, 2 * BLK), lambda p, s: (0, p, 0, 0)),
                pl.BlockSpec((PP, 3 * NT, 2 * BLK), lambda p, s: (p, 0, 0)),
                pl.BlockSpec((n, PP, 3 * NT, 2 * BLK), lambda p, s: (0, p, 0, 0)),
            ],
            out_specs=[
                pl.BlockSpec((NS, 2, BLK, W), lambda p, s: (0, 0, 0, p)),
                pl.BlockSpec((NT, 2, BLK, W), lambda p, s: (0, 0, 0, p)),
            ],
            scratch_shapes=[
                pltpu.VMEM((NS, W, BLK), bf16),
                pltpu.VMEM((NS, 2, BLK, W), f32),
                pltpu.VMEM((PP, 3 * NT, 2 * BLK), f32),
            ],
        ),
        out_shape=[
            jax.ShapeDtypeStruct((NS, 2, BLK, width), bf16),
            jax.ShapeDtypeStruct((NT, 2, BLK, width), bf16),
        ],
        compiler_params=pltpu.CompilerParams(vmem_limit_bytes=VMEM),
        cost_estimate=pl.CostEstimate(
            flops=2 * 10**10, bytes_accessed=30 * 2**20, transcendentals=10**7
        ),
        name="backward",
    )(meta, qg, kv, bias, acc, own, stats)


def tile_lists(adjacency, side):
    on = adjacency > 0
    place = jnp.cumsum(on.astype(jnp.int32), axis=1) - 1
    hit = on[:, None, :] & (place[:, None, :] == jnp.arange(NS)[None, :, None])
    source = jnp.sum(jnp.where(hit, jnp.arange(NS)[None, None, :], 0), axis=2)
    count = jnp.sum(on.astype(jnp.int32), axis=1)
    target = jnp.arange(NT)[:, None]
    base = jnp.where(target // 4 == side, 0, 4 * NS) + target % 4 * NS
    mask = jnp.where(jnp.arange(NS)[None, :] < count[:, None], base + source, EMPTY)
    return jnp.concatenate([count, source.reshape(-1), mask.reshape(-1)]).astype(jnp.int32)


def shards(node_query, node_key, node_value, grad_out, block_adjacency, edge_mask):
    side = lax.axis_index("k")
    swap = [(0, 1), (1, 0)]
    kv = lax.all_gather(jnp.concatenate([node_key, node_value]), ("y", "x"), axis=0, tiled=True)
    kv = kv.reshape(NS, 2, BLK, D)
    qg = lax.all_gather(jnp.concatenate([node_query, grad_out]), ("k", "z"), axis=0, tiled=True)
    qg = qg.reshape(NT, 2, BLK, D)
    own_bias, send_bias = bias_tiles(side.reshape(1), edge_mask)
    got_bias = lax.ppermute(send_bias, "k", swap)
    bias = jnp.concatenate([own_bias, got_bias, jnp.full((1, BLK, BLK), LOW, bf16)])
    by_side = block_adjacency.reshape(4, NS, 2)
    own_adj = jnp.where(side == 0, by_side[..., 0], by_side[..., 1])
    send_adj = jnp.where(side == 0, by_side[..., 1], by_side[..., 0])
    got_adj = lax.ppermute(send_adj, "k", swap)
    adjacency = jnp.where(
        side == 0,
        jnp.concatenate([own_adj, got_adj]),
        jnp.concatenate([got_adj, own_adj]),
    )
    meta = tile_lists(adjacency, side)
    acc, own = forward(meta, qg, kv, bias)
    stats = lax.all_gather(own, ("k", "z"), axis=0)
    dkv, dqa = backward(meta, qg, kv, bias, acc, own, stats)
    dkv = lax.psum_scatter(
        dkv.reshape(NS * 2 * BLK, D), ("y", "x"), scatter_dimension=0, tiled=True
    )
    dqa = lax.psum_scatter(
        dqa.reshape(NT * 2 * BLK, D), ("k", "z"), scatter_dimension=0, tiled=True
    )
    return (dqa[:BLK], dqa[BLK:], dkv[:BLK], dkv[BLK:])


def solution(mesh):
    fine = Mesh(mesh.devices.reshape(4, 4, 2, 4), ("y", "x", "k", "z"))
    row = ("y", "x", "k")
    target = P(row + ("z",), None)
    source = P(("z",) + row, None)
    tile = P(row, "z")
    return jax.shard_map(
        shards,
        mesh=fine,
        in_specs=(target, source, source, target, tile, tile),
        out_specs=(target, target, source, source),
        check_vma=False,
    )
```

```python
import math

import jax
import jax.numpy as jnp
from jax import lax
from jax.experimental import pallas as pl
from jax.experimental.pallas import tpu as pltpu
from jax.sharding import Mesh
from jax.sharding import PartitionSpec as P

D = 1024
HEADS = 16
BLK = 128
HEAD = D // HEADS
HALF = D // 2
NT = 8
NS = 32
MAXT = 32
PP = 2
W = PP * BLK
LOW = -1e30
BASE2 = math.log2(math.e) / math.sqrt(HEAD)
SCALE = 1.0 / math.sqrt(HEAD)
f32 = jnp.float32
bf16 = jnp.bfloat16
VMEM = 58 * 1024 * 1024
EMPTY = 2 * MAXT


def dot(a, b):
    return jnp.dot(a, b, preferred_element_type=f32)


def cols(pp):
    return slice(pp * BLK, (pp + 1) * BLK)


def wide(first, second):
    return jnp.concatenate([first, second], axis=1)


def tall(first, second):
    return jnp.concatenate([first, second], axis=0)


def split_rows(tile):
    lane = lax.broadcasted_iota(jnp.int32, tile.shape, 1)
    zero = jnp.zeros_like(tile)
    return tall(jnp.where(lane < HEAD, tile, zero), jnp.where(lane >= HEAD, tile, zero))


def split_cols(tile):
    turned = tile.T
    zero = jnp.zeros((HEAD, BLK), tile.dtype)
    return wide(tall(turned[:HEAD], zero), tall(zero, turned[HEAD:]))


def bias_kernel(adj, mask_ref, out_ref, slot):
    row = pl.program_id(0)

    @pl.when(row == 0)
    def _():
        slot[0] = 0
        out_ref[...] = jnp.full(out_ref.shape, LOW, bf16)

    for s in range(NS):

        @pl.when(adj[row, s] > 0)
        def _():
            edge = mask_ref[:, s * BLK : (s + 1) * BLK]
            tile = jnp.where(edge > 0, 0.0, LOW).astype(f32)
            out_ref[jnp.minimum(slot[0], MAXT - 1)] = tile.T.astype(bf16)
            slot[0] = slot[0] + 1


def bias_tiles(adjacency, edge_mask):
    return pl.pallas_call(
        bias_kernel,
        grid_spec=pltpu.PrefetchScalarGridSpec(
            num_scalar_prefetch=1,
            grid=(4,),
            in_specs=[pl.BlockSpec((BLK, NS * BLK), lambda i, s: (i, 0))],
            out_specs=pl.BlockSpec((MAXT, BLK, BLK), lambda i, s: (0, 0, 0)),
            scratch_shapes=[pltpu.SMEM((1,), jnp.int32)],
        ),
        out_shape=jax.ShapeDtypeStruct((MAXT, BLK, BLK), bf16),
        compiler_params=pltpu.CompilerParams(vmem_limit_bytes=VMEM),
        cost_estimate=pl.CostEstimate(flops=0, bytes_accessed=30 * 2**20, transcendentals=0),
        name="bias_tiles",
    )(adjacency, edge_mask)


def slots(meta, lt, i):
    count = meta[lt]
    first = meta[NT + lt]
    at = 2 * NT + lt * NS + 2 * i
    b0 = first + 2 * i
    b1 = jnp.where(2 * i + 1 < count, b0 + 1, EMPTY)
    return meta[at], meta[at + 1], b0, b1


def both_bias(bias_ref, b0, b1):
    bias = tall(bias_ref[b0], bias_ref[b1]).astype(f32)
    return wide(bias, bias)


def forward_kernel(meta, qg_ref, kv_ref, bias_ref, acc_ref, stat_ref, vt_ref, score_ref):
    def turn(sb, _):
        for pp in range(PP):
            vt_ref[sb, cols(pp), :] = kv_ref[sb, 1, :, cols(pp)].T
        return 0

    lax.fori_loop(0, NS, turn, 0)

    def target(lt, _):
        queries = [split_cols(qg_ref[lt, 0, :, cols(pp)]) for pp in range(PP)]
        turns = (meta[lt] + 1) // 2

        def score_step(i, tops):
            s0, s1, b0, b1 = slots(meta, lt, i)
            bias = both_bias(bias_ref, b0, b1)
            out = []
            for pp in range(PP):
                keys = tall(kv_ref[s0, 0, :, cols(pp)], kv_ref[s1, 0, :, cols(pp)])
                scores = dot(keys, queries[pp]) * BASE2 + bias
                score_ref[i, pp] = scores
                top = jnp.max(scores.reshape(-1, 8, 2 * BLK), axis=0)
                out.append(jnp.maximum(tops[pp], top))
            return tuple(out)

        tops = lax.fori_loop(
            0, turns, score_step, tuple(jnp.full((8, 2 * BLK), LOW, f32) for _ in range(PP))
        )
        tops = [jnp.max(top, axis=0, keepdims=True) for top in tops]

        def weight_step(i, state):
            s0, s1, _, _ = slots(meta, lt, i)
            out = []
            for pp in range(PP):
                total, acc = state[pp]
                weights = jnp.exp2(score_ref[i, pp] - tops[pp])
                total = total + jnp.sum(weights.reshape(-1, 8, 2 * BLK), axis=0)
                low = weights.astype(bf16)
                vt = wide(vt_ref[s0, cols(pp), :], vt_ref[s1, cols(pp), :])
                part = wide(dot(vt[:HEAD], low[:, :BLK]), dot(vt[HEAD:], low[:, BLK:]))
                out.append((total, acc + part))
            return tuple(out)

        start = tuple(
            (jnp.zeros((8, 2 * BLK), f32), jnp.zeros((HEAD, 2 * BLK), f32)) for _ in range(PP)
        )
        state = lax.fori_loop(0, turns, weight_step, start)
        for pp in range(PP):
            total, acc = state[pp]
            grad = qg_ref[lt, 1, :, cols(pp)].T.astype(f32)
            grad = wide(grad[:HEAD], grad[HEAD:])
            acc_ref[lt, pp] = acc
            stat_ref[pp, pl.ds(lt, 1), :] = tops[pp]
            stat_ref[pp, pl.ds(NT + lt, 1), :] = jnp.sum(total, axis=0, keepdims=True)
            stat_ref[pp, pl.ds(2 * NT + lt, 1), :] = jnp.sum(acc * grad, axis=0, keepdims=True)
        return 0

    lax.fori_loop(0, NT, target, 0)


QG_SPEC = pl.BlockSpec((NT, 2, BLK, W), lambda p, s: (0, 0, 0, p))
KV_SPEC = pl.BlockSpec((NS, 2, BLK, W), lambda p, s: (0, 0, 0, p))
BIAS_SPEC = pl.BlockSpec((EMPTY + 1, BLK, BLK), lambda p, s: (0, 0, 0))
ACC_SPEC = pl.BlockSpec((NT, PP, HEAD, 2 * BLK), lambda p, s: (0, p, 0, 0))
STAT_SPEC = pl.BlockSpec((PP, 3 * NT, 2 * BLK), lambda p, s: (p, 0, 0))


def forward(meta, qg, kv, bias):
    groups = qg.shape[-1] // W
    return pl.pallas_call(
        forward_kernel,
        grid_spec=pltpu.PrefetchScalarGridSpec(
            num_scalar_prefetch=1,
            grid=(groups,),
            in_specs=[QG_SPEC, KV_SPEC, BIAS_SPEC],
            out_specs=[ACC_SPEC, STAT_SPEC],
            scratch_shapes=[
                pltpu.VMEM((NS, W, BLK), bf16),
                pltpu.VMEM((NS // 2, PP, 2 * BLK, 2 * BLK), f32),
            ],
        ),
        out_shape=[
            jax.ShapeDtypeStruct((NT, groups * PP, HEAD, 2 * BLK), f32),
            jax.ShapeDtypeStruct((groups * PP, 3 * NT, 2 * BLK), f32),
        ],
        compiler_params=pltpu.CompilerParams(vmem_limit_bytes=VMEM),
        cost_estimate=pl.CostEstimate(
            flops=10**10, bytes_accessed=20 * 2**20, transcendentals=10**7
        ),
        name="forward",
    )(meta, qg, kv, bias)


def backward_kernel(
    meta, qg_ref, kv_ref, bias_ref, acc_ref, own_ref, one_ref, two_ref, three_ref,
    dkv_ref, dqa_ref, kt_ref, sum_ref, row_ref,
):
    def turn(sb, _):
        for pp in range(PP):
            kt_ref[sb, cols(pp), :] = kv_ref[sb, 0, :, cols(pp)].T
        return 0

    lax.fori_loop(0, NS, turn, 0)
    sum_ref[...] = jnp.zeros_like(sum_ref)
    for pp in range(PP):
        parts = []
        for back, ref in enumerate((own_ref, one_ref, two_ref, three_ref)):
            stat = [ref[pp, part * NT : (part + 1) * NT, :] for part in range(3)]
            if back:
                stat = [pltpu.roll(rows, 2 * back, 0) for rows in stat]
            parts.append(stat)
        top = jnp.maximum(
            jnp.maximum(parts[0][0], parts[1][0]), jnp.maximum(parts[2][0], parts[3][0])
        )
        factors = [jnp.exp2(stat[0] - top) for stat in parts]
        total = sum(stat[1] * factor for stat, factor in zip(parts, factors))
        delta = sum(stat[2] * factor for stat, factor in zip(parts, factors))
        log_total = top + jnp.log2(total)
        row_ref[pp, :NT, :] = log_total
        row_ref[pp, NT : 2 * NT, :] = delta / total
        row_ref[pp, 2 * NT :, :] = jnp.exp2(parts[0][0] - log_total)

    def target(lt, _):
        tiles = [
            (qg_ref[lt, 0, :, cols(pp)], qg_ref[lt, 1, :, cols(pp)]) for pp in range(PP)
        ]
        rows = [(split_rows(query), split_rows(grad)) for query, grad in tiles]
        turned = [(split_cols(query), split_cols(grad)) for query, grad in tiles]
        log_totals = [row_ref[pp, pl.ds(lt, 1), :] for pp in range(PP)]
        deltas = [row_ref[pp, pl.ds(NT + lt, 1), :] for pp in range(PP)]

        def step(i, state):
            s0, s1, b0, b1 = slots(meta, lt, i)
            bias = both_bias(bias_ref, b0, b1)
            out = []
            for pp in range(PP):
                keys = tall(kv_ref[s0, 0, :, cols(pp)], kv_ref[s1, 0, :, cols(pp)])
                values = tall(kv_ref[s0, 1, :, cols(pp)], kv_ref[s1, 1, :, cols(pp)])
                scores = dot(keys, turned[pp][0]) * BASE2 + bias
                probs = jnp.exp2(scores - log_totals[pp])
                grad_prob = dot(values, turned[pp][1])
                grad_score = (probs * (grad_prob - deltas[pp])).astype(bf16)
                value_part = dot(probs.astype(bf16), rows[pp][1])
                key_part = dot(grad_score, rows[pp][0])
                sum_ref[s0, 0, :, cols(pp)] += key_part[:BLK]
                sum_ref[s1, 0, :, cols(pp)] += key_part[BLK:]
                sum_ref[s0, 1, :, cols(pp)] += value_part[:BLK]
                sum_ref[s1, 1, :, cols(pp)] += value_part[BLK:]
                kt = wide(kt_ref[s0, cols(pp), :], kt_ref[s1, cols(pp), :])
                part = wide(
                    dot(kt[:HEAD], grad_score[:, :BLK]), dot(kt[HEAD:], grad_score[:, BLK:])
                )
                out.append(state[pp] + part)
            return tuple(out)

        start = tuple(jnp.zeros((HEAD, 2 * BLK), f32) for _ in range(PP))
        state = lax.fori_loop(0, (meta[lt] + 1) // 2, step, start)
        for pp in range(PP):
            attended = acc_ref[lt, pp] * row_ref[pp, pl.ds(2 * NT + lt, 1), :]
            attended = tall(attended[:, :BLK], attended[:, BLK:])
            query_grad = tall(state[pp][:, :BLK], state[pp][:, BLK:]) * SCALE
            dqa_ref[lt, 0, :, cols(pp)] = attended.T.astype(bf16)
            dqa_ref[lt, 1, :, cols(pp)] = query_grad.T.astype(bf16)
        return 0

    lax.fori_loop(0, NT, target, 0)
    dkv_ref[:, 0] = (sum_ref[:, 0] * SCALE).astype(bf16)
    dkv_ref[:, 1] = sum_ref[:, 1].astype(bf16)


def backward(meta, qg, kv, bias, acc, stats):
    groups = qg.shape[-1] // W
    width = groups * W
    return pl.pallas_call(
        backward_kernel,
        grid_spec=pltpu.PrefetchScalarGridSpec(
            num_scalar_prefetch=1,
            grid=(groups,),
            in_specs=[QG_SPEC, KV_SPEC, BIAS_SPEC, ACC_SPEC] + [STAT_SPEC] * 4,
            out_specs=[KV_SPEC, QG_SPEC],
            scratch_shapes=[
                pltpu.VMEM((NS, W, BLK), bf16),
                pltpu.VMEM((NS, 2, BLK, W), f32),
                pltpu.VMEM((PP, 3 * NT, 2 * BLK), f32),
            ],
        ),
        out_shape=[
            jax.ShapeDtypeStruct((NS, 2, BLK, width), bf16),
            jax.ShapeDtypeStruct((NT, 2, BLK, width), bf16),
        ],
        compiler_params=pltpu.CompilerParams(vmem_limit_bytes=VMEM),
        cost_estimate=pl.CostEstimate(
            flops=2 * 10**10, bytes_accessed=30 * 2**20, transcendentals=10**7
        ),
        name="backward",
    )(meta, qg, kv, bias, acc, *stats)


def steps_back(rows, z):
    turned = jnp.concatenate([rows[:1], rows[3:], rows[2:3], rows[1:2]])
    return lax.dynamic_slice_in_dim(jnp.concatenate([turned, turned]), 4 - z, 4)


def tile_lists(own_adj, got_adj, side, z):
    adj = jnp.stack([own_adj, got_adj], axis=1)
    count = jnp.sum(adj, axis=2)
    first = jnp.cumsum(count, axis=0) - count + jnp.array([0, MAXT])
    adj = steps_back(adj, z).reshape(NT, NS)
    count = steps_back(count, z).reshape(NT)
    first = steps_back(first, z).reshape(NT)
    place = jnp.cumsum(adj, axis=1) - 1
    hit = (adj[:, None, :] > 0) & (place[:, None, :] == jnp.arange(NS)[None, :, None])
    held = jnp.arange(NS) ^ side
    source = jnp.sum(jnp.where(hit, held[None, None, :], 0), axis=2)
    return jnp.concatenate([count, first, source.reshape(-1)]).astype(jnp.int32)


SWAP = [(0, 1), (1, 0)]


def back(array, steps):
    return lax.ppermute(array, "z", [(s, (s + steps) % 4) for s in range(4)])


def half(array, side):
    return lax.dynamic_slice_in_dim(array, side * HALF, HALF, array.ndim - 1)


def chip_pair(first, second, side):
    both = jnp.concatenate([first, second])
    got = lax.ppermute(half(both, 1 - side), "k", SWAP)
    return jnp.concatenate([half(both, side), got])


def own_blocks(pair, side):
    got = lax.ppermute(pair[1], "k", SWAP)
    whole = jnp.where(
        side == 0,
        jnp.concatenate([pair[0], got], axis=-1),
        jnp.concatenate([got, pair[0]], axis=-1),
    )
    return whole[0], whole[1]


def shards(node_query, node_key, node_value, grad_out, block_adjacency, edge_mask):
    side = lax.axis_index("k")
    z = lax.axis_index("z")
    kv = lax.all_gather(chip_pair(node_key, node_value, side), ("y", "x"), axis=0, tiled=True)
    kv = kv.reshape(NS, 2, BLK, HALF)
    qg = chip_pair(node_query, grad_out, side)
    qg = jnp.concatenate([qg] + [back(qg, steps) for steps in (1, 2, 3)])
    qg = qg.reshape(NT, 2, BLK, HALF)
    own_adj = (block_adjacency > 0).astype(jnp.int32)
    own_bias = bias_tiles(own_adj, edge_mask)
    got_bias = lax.ppermute(own_bias, "k", SWAP)
    bias = jnp.concatenate([own_bias, got_bias, jnp.full((1, BLK, BLK), LOW, bf16)])
    got_adj = lax.ppermute(own_adj, "k", SWAP)
    meta = tile_lists(own_adj, got_adj, side, z)
    acc, own = forward(meta, qg, kv, bias)
    stats = [own] + [back(own, steps) for steps in (1, 2, 3)]
    dkv, dqa = backward(meta, qg, kv, bias, acc, stats)
    dkv = lax.psum_scatter(
        dkv.reshape(NS * 2 * BLK, HALF), ("y", "x"), scatter_dimension=0, tiled=True
    )
    dqa = dqa.reshape(4, 2, 2, BLK, HALF)
    summed = dqa[0].astype(f32)
    for steps in (1, 2, 3):
        summed = summed + back(dqa[steps], -steps).astype(f32)
    attended, grad_query = own_blocks(summed.astype(bf16), side)
    grad_key, grad_value = own_blocks(dkv.reshape(2, 2, BLK, HALF), side)
    return (attended, grad_query, grad_key, grad_value)


def solution(mesh):
    fine = Mesh(mesh.devices.reshape(4, 4, 2, 4), ("y", "x", "k", "z"))
    row = ("y", "x", "k")
    target = P(row + ("z",), None)
    source = P(("z",) + row, None)
    tile = P(row, "z")
    return jax.shard_map(
        shards,
        mesh=fine,
        in_specs=(target, source, source, target, tile, tile),
        out_specs=(target, target, source, source),
        check_vma=False,
    )
```

```python
import math

import jax
import jax.numpy as jnp
from jax import lax
from jax.experimental import pallas as pl
from jax.experimental.pallas import tpu as pltpu
from jax.sharding import Mesh
from jax.sharding import PartitionSpec as P

D = 1024
HEADS = 16
BLK = 128
HEAD = D // HEADS
QUAD = 4
PART = D // QUAD
NT = 4 * QUAD
NS = 32
MAXT = 32
PP = 2
W = PP * BLK
LOW = -1e30
BASE2 = math.log2(math.e) / math.sqrt(HEAD)
SCALE = 1.0 / math.sqrt(HEAD)
f32 = jnp.float32
bf16 = jnp.bfloat16
VMEM = 58 * 1024 * 1024


def dot(a, b):
    return jnp.dot(a, b, preferred_element_type=f32)


def cols(pp):
    return slice(pp * BLK, (pp + 1) * BLK)


def wide(first, second):
    return jnp.concatenate([first, second], axis=1)


def tall(first, second):
    return jnp.concatenate([first, second], axis=0)


def split_rows(tile):
    lane = lax.broadcasted_iota(jnp.int32, tile.shape, 1)
    zero = jnp.zeros_like(tile)
    return tall(jnp.where(lane < HEAD, tile, zero), jnp.where(lane >= HEAD, tile, zero))


def split_cols(tile):
    turned = tile.T
    zero = jnp.zeros((HEAD, BLK), tile.dtype)
    return wide(tall(turned[:HEAD], zero), tall(zero, turned[HEAD:]))


def bias_kernel(adj, mask_ref, out_ref, slot):
    row = pl.program_id(0)

    @pl.when(row == 0)
    def _():
        slot[0] = 0
        out_ref[...] = jnp.full(out_ref.shape, LOW, bf16)

    for s in range(NS):

        @pl.when(adj[row, s] > 0)
        def _():
            edge = mask_ref[:, s * BLK : (s + 1) * BLK]
            tile = jnp.where(edge > 0, 0.0, LOW).astype(f32)
            out_ref[jnp.minimum(slot[0], MAXT - 1)] = tile.T.astype(bf16)
            slot[0] = slot[0] + 1


def bias_tiles(adjacency, edge_mask):
    return pl.pallas_call(
        bias_kernel,
        grid_spec=pltpu.PrefetchScalarGridSpec(
            num_scalar_prefetch=1,
            grid=(4,),
            in_specs=[pl.BlockSpec((BLK, NS * BLK), lambda i, s: (i, 0))],
            out_specs=pl.BlockSpec((MAXT, BLK, BLK), lambda i, s: (0, 0, 0)),
            scratch_shapes=[pltpu.SMEM((1,), jnp.int32)],
        ),
        out_shape=jax.ShapeDtypeStruct((MAXT, BLK, BLK), bf16),
        compiler_params=pltpu.CompilerParams(vmem_limit_bytes=VMEM),
        cost_estimate=pl.CostEstimate(flops=0, bytes_accessed=30 * 2**20, transcendentals=0),
        name="bias_tiles",
    )(adjacency, edge_mask)


def sources(meta, lt, i):
    at = 2 * NT + lt * NS + 2 * i
    return meta[at], meta[at + 1]


def step_bias(meta, near_ref, far_ref, lt, i):
    near = lax.rem(lt, QUAD) < QUAD // 2
    at = meta[NT + lt] + 2 * i
    there = 2 * i + 1 < meta[lt]
    after = jnp.where(there, at + 1, at)
    first = jnp.where(near, near_ref[at], far_ref[at]).astype(f32)
    second = jnp.where(near, near_ref[after], far_ref[after]).astype(f32)
    bias = tall(first, jnp.where(there, second, LOW))
    return wide(bias, bias)


def forward_kernel(meta, qg_ref, kv_ref, near_ref, far_ref, acc_ref, stat_ref, vt_ref, score_ref):
    def turn(sb, _):
        for pp in range(PP):
            vt_ref[sb, cols(pp), :] = kv_ref[sb, 1, :, cols(pp)].T
        return 0

    lax.fori_loop(0, NS, turn, 0)

    def target(lt, _):
        queries = [split_cols(qg_ref[lt, 0, :, cols(pp)]) for pp in range(PP)]
        turns = (meta[lt] + 1) // 2

        def score_step(i, tops):
            s0, s1 = sources(meta, lt, i)
            bias = step_bias(meta, near_ref, far_ref, lt, i)
            out = []
            for pp in range(PP):
                keys = tall(kv_ref[s0, 0, :, cols(pp)], kv_ref[s1, 0, :, cols(pp)])
                scores = dot(keys, queries[pp]) * BASE2 + bias
                score_ref[i, pp] = scores
                top = jnp.max(scores.reshape(-1, 8, 2 * BLK), axis=0)
                out.append(jnp.maximum(tops[pp], top))
            return tuple(out)

        tops = lax.fori_loop(
            0, turns, score_step, tuple(jnp.full((8, 2 * BLK), LOW, f32) for _ in range(PP))
        )
        tops = [jnp.max(top, axis=0, keepdims=True) for top in tops]

        def weight_step(i, state):
            s0, s1 = sources(meta, lt, i)
            out = []
            for pp in range(PP):
                total, acc = state[pp]
                weights = jnp.exp2(score_ref[i, pp] - tops[pp])
                total = total + jnp.sum(weights.reshape(-1, 8, 2 * BLK), axis=0)
                low = weights.astype(bf16)
                vt = wide(vt_ref[s0, cols(pp), :], vt_ref[s1, cols(pp), :])
                part = wide(dot(vt[:HEAD], low[:, :BLK]), dot(vt[HEAD:], low[:, BLK:]))
                out.append((total, acc + part))
            return tuple(out)

        start = tuple(
            (jnp.zeros((8, 2 * BLK), f32), jnp.zeros((HEAD, 2 * BLK), f32)) for _ in range(PP)
        )
        state = lax.fori_loop(0, turns, weight_step, start)
        for pp in range(PP):
            total, acc = state[pp]
            grad = qg_ref[lt, 1, :, cols(pp)].T.astype(f32)
            grad = wide(grad[:HEAD], grad[HEAD:])
            acc_ref[lt, pp] = acc
            stat_ref[pp, pl.ds(lt, 1), :] = tops[pp]
            stat_ref[pp, pl.ds(NT + lt, 1), :] = jnp.sum(total, axis=0, keepdims=True)
            stat_ref[pp, pl.ds(2 * NT + lt, 1), :] = jnp.sum(acc * grad, axis=0, keepdims=True)
        return 0

    lax.fori_loop(0, NT, target, 0)


QG_SPEC = pl.BlockSpec((NT, 2, BLK, W), lambda p, s: (0, 0, 0, p))
KV_SPEC = pl.BlockSpec((NS, 2, BLK, W), lambda p, s: (0, 0, 0, p))
BIAS_SPEC = pl.BlockSpec((QUAD // 2 * MAXT, BLK, BLK), lambda p, s: (0, 0, 0))
ACC_SPEC = pl.BlockSpec((NT, PP, HEAD, 2 * BLK), lambda p, s: (0, p, 0, 0))
STAT_SPEC = pl.BlockSpec((PP, 3 * NT, 2 * BLK), lambda p, s: (p, 0, 0))


def forward(meta, qg, kv, near, far):
    groups = qg.shape[-1] // W
    return pl.pallas_call(
        forward_kernel,
        grid_spec=pltpu.PrefetchScalarGridSpec(
            num_scalar_prefetch=1,
            grid=(groups,),
            in_specs=[QG_SPEC, KV_SPEC, BIAS_SPEC, BIAS_SPEC],
            out_specs=[ACC_SPEC, STAT_SPEC],
            scratch_shapes=[
                pltpu.VMEM((NS, W, BLK), bf16),
                pltpu.VMEM((NS // 2, PP, 2 * BLK, 2 * BLK), f32),
            ],
        ),
        out_shape=[
            jax.ShapeDtypeStruct((NT, groups * PP, HEAD, 2 * BLK), f32),
            jax.ShapeDtypeStruct((groups * PP, 3 * NT, 2 * BLK), f32),
        ],
        compiler_params=pltpu.CompilerParams(vmem_limit_bytes=VMEM),
        cost_estimate=pl.CostEstimate(
            flops=10**10, bytes_accessed=20 * 2**20, transcendentals=10**7
        ),
        name="forward",
    )(meta, qg, kv, near, far)


def backward_kernel(
    meta, qg_ref, kv_ref, near_ref, far_ref, acc_ref, own_ref, one_ref, two_ref, three_ref,
    dkv_ref, dqa_ref, kt_ref, sum_ref, row_ref,
):
    def turn(sb, _):
        for pp in range(PP):
            kt_ref[sb, cols(pp), :] = kv_ref[sb, 0, :, cols(pp)].T
        return 0

    lax.fori_loop(0, NS, turn, 0)
    sum_ref[...] = jnp.zeros_like(sum_ref)
    for pp in range(PP):
        parts = []
        for back, ref in enumerate((own_ref, one_ref, two_ref, three_ref)):
            stat = [ref[pp, part * NT : (part + 1) * NT, :] for part in range(3)]
            if back:
                stat = [pltpu.roll(rows, QUAD * back, 0) for rows in stat]
            parts.append(stat)
        top = jnp.maximum(
            jnp.maximum(parts[0][0], parts[1][0]), jnp.maximum(parts[2][0], parts[3][0])
        )
        factors = [jnp.exp2(stat[0] - top) for stat in parts]
        total = sum(stat[1] * factor for stat, factor in zip(parts, factors))
        delta = sum(stat[2] * factor for stat, factor in zip(parts, factors))
        log_total = top + jnp.log2(total)
        row_ref[pp, :NT, :] = log_total
        row_ref[pp, NT : 2 * NT, :] = delta / total
        row_ref[pp, 2 * NT :, :] = jnp.exp2(parts[0][0] - log_total)

    def target(lt, _):
        tiles = [
            (qg_ref[lt, 0, :, cols(pp)], qg_ref[lt, 1, :, cols(pp)]) for pp in range(PP)
        ]
        rows = [(split_rows(query), split_rows(grad)) for query, grad in tiles]
        turned = [(split_cols(query), split_cols(grad)) for query, grad in tiles]
        log_totals = [row_ref[pp, pl.ds(lt, 1), :] for pp in range(PP)]
        deltas = [row_ref[pp, pl.ds(NT + lt, 1), :] for pp in range(PP)]

        def step(i, state):
            s0, s1 = sources(meta, lt, i)
            bias = step_bias(meta, near_ref, far_ref, lt, i)
            out = []
            for pp in range(PP):
                keys = tall(kv_ref[s0, 0, :, cols(pp)], kv_ref[s1, 0, :, cols(pp)])
                values = tall(kv_ref[s0, 1, :, cols(pp)], kv_ref[s1, 1, :, cols(pp)])
                scores = dot(keys, turned[pp][0]) * BASE2 + bias
                probs = jnp.exp2(scores - log_totals[pp])
                grad_prob = dot(values, turned[pp][1])
                grad_score = (probs * (grad_prob - deltas[pp])).astype(bf16)
                value_part = dot(probs.astype(bf16), rows[pp][1])
                key_part = dot(grad_score, rows[pp][0])
                sum_ref[s0, 0, :, cols(pp)] += key_part[:BLK]
                sum_ref[s1, 0, :, cols(pp)] += key_part[BLK:]
                sum_ref[s0, 1, :, cols(pp)] += value_part[:BLK]
                sum_ref[s1, 1, :, cols(pp)] += value_part[BLK:]
                kt = wide(kt_ref[s0, cols(pp), :], kt_ref[s1, cols(pp), :])
                part = wide(
                    dot(kt[:HEAD], grad_score[:, :BLK]), dot(kt[HEAD:], grad_score[:, BLK:])
                )
                out.append(state[pp] + part)
            return tuple(out)

        start = tuple(jnp.zeros((HEAD, 2 * BLK), f32) for _ in range(PP))
        state = lax.fori_loop(0, (meta[lt] + 1) // 2, step, start)
        for pp in range(PP):
            attended = acc_ref[lt, pp] * row_ref[pp, pl.ds(2 * NT + lt, 1), :]
            attended = tall(attended[:, :BLK], attended[:, BLK:])
            query_grad = tall(state[pp][:, :BLK], state[pp][:, BLK:]) * SCALE
            dqa_ref[lt, 0, :, cols(pp)] = attended.T.astype(bf16)
            dqa_ref[lt, 1, :, cols(pp)] = query_grad.T.astype(bf16)
        return 0

    lax.fori_loop(0, NT, target, 0)
    dkv_ref[:, 0] = (sum_ref[:, 0] * SCALE).astype(bf16)
    dkv_ref[:, 1] = sum_ref[:, 1].astype(bf16)


def backward(meta, qg, kv, near, far, acc, stats):
    groups = qg.shape[-1] // W
    width = groups * W
    return pl.pallas_call(
        backward_kernel,
        grid_spec=pltpu.PrefetchScalarGridSpec(
            num_scalar_prefetch=1,
            grid=(groups,),
            in_specs=[QG_SPEC, KV_SPEC, BIAS_SPEC, BIAS_SPEC, ACC_SPEC] + [STAT_SPEC] * 4,
            out_specs=[KV_SPEC, QG_SPEC],
            scratch_shapes=[
                pltpu.VMEM((NS, W, BLK), bf16),
                pltpu.VMEM((NS, 2, BLK, W), f32),
                pltpu.VMEM((PP, 3 * NT, 2 * BLK), f32),
            ],
        ),
        out_shape=[
            jax.ShapeDtypeStruct((NS, 2, BLK, width), bf16),
            jax.ShapeDtypeStruct((NT, 2, BLK, width), bf16),
        ],
        compiler_params=pltpu.CompilerParams(vmem_limit_bytes=VMEM),
        cost_estimate=pl.CostEstimate(
            flops=2 * 10**10, bytes_accessed=30 * 2**20, transcendentals=10**7
        ),
        name="backward",
    )(meta, qg, kv, near, far, acc, *stats)


def steps_back(rows, z):
    turned = jnp.concatenate([rows[:1], rows[3:], rows[2:3], rows[1:2]])
    return lax.dynamic_slice_in_dim(jnp.concatenate([turned, turned]), 4 - z, 4)


def tile_lists(adj, side, near, z):
    adj = adj.transpose(1, 0, 2)
    count = jnp.sum(adj, axis=2)
    first = jnp.cumsum(count, axis=0) - count + jnp.arange(QUAD) % 2 * MAXT
    adj = steps_back(adj, z).reshape(NT, NS)
    count = steps_back(count, z).reshape(NT)
    first = steps_back(first, z).reshape(NT)
    place = jnp.cumsum(adj, axis=1) - 1
    hit = (adj[:, None, :] > 0) & (place[:, None, :] == jnp.arange(NS)[None, :, None])
    index = jnp.arange(NS)
    held = index // QUAD * QUAD + 2 * (index % 2 ^ side) + (index // 2 % 2 ^ near)
    source = jnp.sum(jnp.where(hit, held[None, None, :], 0), axis=2)
    return jnp.concatenate([count, first, source.reshape(-1)]).astype(jnp.int32)


SWAP = [(0, 1), (1, 0)]


def back(array, steps):
    return lax.ppermute(array, "z", [(s, (s + steps) % 4) for s in range(4)])


def other(array, axis):
    return lax.ppermute(array, axis, SWAP)


def half(array, index):
    size = array.shape[-1] // 2
    return lax.dynamic_slice_in_dim(array, index * size, size, array.ndim - 1)


def quad_part(first, second, side, near):
    both = jnp.stack([first, second])
    both = jnp.stack([half(both, near), other(half(both, 1 - near), "xl")])
    return jnp.concatenate([half(both, side), other(half(both, 1 - side), "k")])


def join(mine, got, index):
    return jnp.where(
        index == 0,
        jnp.concatenate([mine, got], axis=-1),
        jnp.concatenate([got, mine], axis=-1),
    )


def own_blocks(part, side, near):
    both = join(part[:2], other(part[2:], "k"), side)
    whole = join(both[0], other(both[1], "xl"), near)
    return whole[0], whole[1]


def shards(node_query, node_key, node_value, grad_out, block_adjacency, edge_mask):
    side, near, z = (lax.axis_index(axis) for axis in ("k", "xl", "z"))
    kv = quad_part(node_key, node_value, side, near).reshape(QUAD * 2 * BLK, PART)
    kv = lax.all_gather(kv, ("y", "xh"), axis=0, tiled=True).reshape(NS, 2, BLK, PART)
    qg = quad_part(node_query, grad_out, side, near).reshape(QUAD * 2 * BLK, PART)
    qg = jnp.concatenate([qg] + [back(qg, steps) for steps in (1, 2, 3)])
    qg = qg.reshape(NT, 2, BLK, PART)
    own_adj = (block_adjacency > 0).astype(jnp.int32)
    own_bias = bias_tiles(own_adj, edge_mask)
    near_bias = jnp.concatenate([own_bias, other(own_bias, "xl")])
    far_bias = other(near_bias, "k")
    adj = jnp.stack([own_adj, other(own_adj, "xl")])
    adj = jnp.concatenate([adj, other(adj, "k")])
    meta = tile_lists(adj, side, near, z)
    acc, own = forward(meta, qg, kv, near_bias, far_bias)
    stats = [own] + [back(own, steps) for steps in (1, 2, 3)]
    dkv, dqa = backward(meta, qg, kv, near_bias, far_bias, acc, stats)
    dkv = lax.psum_scatter(
        dkv.reshape(NS * 2 * BLK, PART), ("y", "xh"), scatter_dimension=0, tiled=True
    )
    dqa = dqa.reshape(4, QUAD, 2, BLK, PART)
    summed = dqa[0].astype(f32)
    for steps in (1, 2, 3):
        summed = summed + back(dqa[steps], -steps).astype(f32)
    attended, grad_query = own_blocks(summed.astype(bf16), side, near)
    grad_key, grad_value = own_blocks(dkv.reshape(QUAD, 2, BLK, PART), side, near)
    return (attended, grad_query, grad_key, grad_value)


def solution(mesh):
    fine = Mesh(mesh.devices.reshape(4, 2, 2, 2, 4), ("y", "xh", "xl", "k", "z"))
    row = ("y", "xh", "xl", "k")
    target = P(row + ("z",), None)
    source = P(("z",) + row, None)
    tile = P(row, "z")
    return jax.shard_map(
        shards,
        mesh=fine,
        in_specs=(target, source, source, target, tile, tile),
        out_specs=(target, target, source, source),
        check_vma=False,
    )
```

```python
import functools
import math

import jax
import jax.numpy as jnp
from jax import lax
from jax.experimental import pallas as pl
from jax.experimental.pallas import tpu as pltpu
from jax.sharding import Mesh
from jax.sharding import PartitionSpec as P

D = 1024
HEADS = 16
BLK = 128
HEAD = D // HEADS
HALF = D // 2
NT = 8
NS = 32
CHIPS = NS // 2
MAXT = 32
PP = 2
W = PP * BLK
LOW = -1e30
BASE2 = math.log2(math.e) / math.sqrt(HEAD)
SCALE = 1.0 / math.sqrt(HEAD)
f32 = jnp.float32
bf16 = jnp.bfloat16
VMEM = 48 * 1024 * 1024
EMPTY = 2 * MAXT


def dot(a, b):
    return jnp.dot(a, b, preferred_element_type=f32)


def cols(pp):
    return slice(pp * BLK, (pp + 1) * BLK)


def wide(first, second):
    return jnp.concatenate([first, second], axis=1)


def tall(first, second):
    return jnp.concatenate([first, second], axis=0)


def split_rows(tile):
    lane = lax.broadcasted_iota(jnp.int32, tile.shape, 1)
    zero = jnp.zeros_like(tile)
    return tall(jnp.where(lane < HEAD, tile, zero), jnp.where(lane >= HEAD, tile, zero))


def split_cols(tile):
    turned = tile.T
    zero = jnp.zeros((HEAD, BLK), tile.dtype)
    return wide(tall(turned[:HEAD], zero), tall(zero, turned[HEAD:]))


def bias_kernel(adj, mask_ref, out_ref, slot):
    row = pl.program_id(0)

    @pl.when(row == 0)
    def _():
        slot[0] = 0
        out_ref[...] = jnp.full(out_ref.shape, LOW, bf16)

    for s in range(NS):

        @pl.when(adj[row, s] > 0)
        def _():
            edge = mask_ref[:, s * BLK : (s + 1) * BLK]
            tile = jnp.where(edge > 0, 0.0, LOW).astype(f32)
            out_ref[jnp.minimum(slot[0], MAXT - 1)] = tile.T.astype(bf16)
            slot[0] = slot[0] + 1


def bias_tiles(adjacency, edge_mask):
    return pl.pallas_call(
        bias_kernel,
        grid_spec=pltpu.PrefetchScalarGridSpec(
            num_scalar_prefetch=1,
            grid=(4,),
            in_specs=[pl.BlockSpec((BLK, NS * BLK), lambda i, s: (i, 0))],
            out_specs=pl.BlockSpec((MAXT, BLK, BLK), lambda i, s: (0, 0, 0)),
            scratch_shapes=[pltpu.SMEM((1,), jnp.int32)],
        ),
        out_shape=jax.ShapeDtypeStruct((MAXT, BLK, BLK), bf16),
        compiler_params=pltpu.CompilerParams(vmem_limit_bytes=VMEM),
        cost_estimate=pl.CostEstimate(flops=0, bytes_accessed=30 * 2**20, transcendentals=0),
        name="bias_tiles",
    )(adjacency, edge_mask)


ABSOLUTE, RELATIVE_KEY, RELATIVE_VALUE = range(3)


def block(meta, order, lt, slot):
    index = meta[2 * NT + (order * NT + lt) * NS + slot]
    return index // 2, index % 2


def pair(meta, order, lt, i):
    return block(meta, order, lt, 2 * i), block(meta, order, lt, 2 * i + 1)


def masks(meta, lt, i):
    first = meta[NT + lt] + 2 * i
    return first, jnp.where(2 * i + 1 < meta[lt], first + 1, EMPTY)


def orders(relative):
    return (RELATIVE_KEY, RELATIVE_VALUE) if relative else (ABSOLUTE, ABSOLUTE)


def both_bias(bias_ref, b0, b1):
    bias = tall(bias_ref[b0], bias_ref[b1]).astype(f32)
    return wide(bias, bias)


def turn_blocks(turned_ref, ref):
    def turn(chip, _):
        for member in range(2):
            for pp in range(PP):
                turned_ref[chip, member, cols(pp), :] = ref[chip, member, :, cols(pp)].T
        return 0

    lax.fori_loop(0, CHIPS, turn, 0)


def rows_of(ref, blocks, pp):
    (c0, m0), (c1, m1) = blocks
    return tall(ref[c0, m0, :, cols(pp)], ref[c1, m1, :, cols(pp)])


def turned_of(ref, blocks, pp):
    (c0, m0), (c1, m1) = blocks
    return wide(ref[c0, m0, cols(pp), :], ref[c1, m1, cols(pp), :])


def add_rows(ref, blocks, kind, pp, part):
    for (chip, member), rows in zip(blocks, (part[:BLK], part[BLK:])):
        ref[kind, chip, member, :, cols(pp)] += rows


def forward_kernel(
    order, meta, qg_ref, key_ref, value_ref, bias_ref, acc_ref, stat_ref, vt_ref, score_ref
):
    turn_blocks(vt_ref, value_ref)

    def target(lt, _):
        queries = [split_cols(qg_ref[lt, 0, :, cols(pp)]) for pp in range(PP)]
        turns = (meta[lt] + 1) // 2

        def score_step(i, tops):
            blocks = pair(meta, order[0], lt, i)
            bias = both_bias(bias_ref, *masks(meta, lt, i))
            out = []
            for pp in range(PP):
                keys = rows_of(key_ref, blocks, pp)
                scores = dot(keys, queries[pp]) * BASE2 + bias
                score_ref[i, pp] = scores
                top = jnp.max(scores.reshape(-1, 8, 2 * BLK), axis=0)
                out.append(jnp.maximum(tops[pp], top))
            return tuple(out)

        tops = lax.fori_loop(
            0, turns, score_step, tuple(jnp.full((8, 2 * BLK), LOW, f32) for _ in range(PP))
        )
        tops = [jnp.max(top, axis=0, keepdims=True) for top in tops]

        def weight_step(i, state):
            blocks = pair(meta, order[1], lt, i)
            out = []
            for pp in range(PP):
                total, acc = state[pp]
                weights = jnp.exp2(score_ref[i, pp] - tops[pp])
                total = total + jnp.sum(weights.reshape(-1, 8, 2 * BLK), axis=0)
                low = weights.astype(bf16)
                vt = turned_of(vt_ref, blocks, pp)
                part = wide(dot(vt[:HEAD], low[:, :BLK]), dot(vt[HEAD:], low[:, BLK:]))
                out.append((total, acc + part))
            return tuple(out)

        start = tuple(
            (jnp.zeros((8, 2 * BLK), f32), jnp.zeros((HEAD, 2 * BLK), f32)) for _ in range(PP)
        )
        state = lax.fori_loop(0, turns, weight_step, start)
        for pp in range(PP):
            total, acc = state[pp]
            grad = qg_ref[lt, 1, :, cols(pp)].T.astype(f32)
            grad = wide(grad[:HEAD], grad[HEAD:])
            acc_ref[lt, pp] = acc
            stat_ref[pp, pl.ds(lt, 1), :] = tops[pp]
            stat_ref[pp, pl.ds(NT + lt, 1), :] = jnp.sum(total, axis=0, keepdims=True)
            stat_ref[pp, pl.ds(2 * NT + lt, 1), :] = jnp.sum(acc * grad, axis=0, keepdims=True)
        return 0

    lax.fori_loop(0, NT, target, 0)


BIAS_SPEC = pl.BlockSpec((EMPTY + 1, BLK, BLK), lambda p, s: (0, 0, 0))
ACC_SPEC = pl.BlockSpec((NT, PP, HEAD, 2 * BLK), lambda p, s: (0, 0, 0, 0))
STAT_SPEC = pl.BlockSpec((PP, 3 * NT, 2 * BLK), lambda p, s: (0, 0, 0))
OUT_SPEC = pl.BlockSpec((NT, 2, BLK, W), lambda p, s: (0, 0, 0, 0))


def qg_spec(group):
    return pl.BlockSpec((NT, 2, BLK, W), lambda p, s: (0, 0, 0, group))


def kv_specs(kv):
    if len(kv) == 2:
        return [pl.BlockSpec((CHIPS, 2, BLK, W), lambda p, s: (0, 0, 0, 0))] * 2
    shape = (CHIPS, None, 2, BLK, W)
    return [
        pl.BlockSpec(shape, lambda p, s: (0, 0, 0, 0, 0)),
        pl.BlockSpec(shape, lambda p, s: (0, 1, 0, 0, 0)),
    ]


def forward(meta, group, qg, kv, bias):
    return pl.pallas_call(
        functools.partial(forward_kernel, orders(len(kv) == 2)),
        grid_spec=pltpu.PrefetchScalarGridSpec(
            num_scalar_prefetch=1,
            grid=(1,),
            in_specs=[qg_spec(group)] + kv_specs(kv) + [BIAS_SPEC],
            out_specs=[ACC_SPEC, STAT_SPEC],
            scratch_shapes=[
                pltpu.VMEM((CHIPS, 2, W, BLK), bf16),
                pltpu.VMEM((NS // 2, PP, 2 * BLK, 2 * BLK), f32),
            ],
        ),
        out_shape=[
            jax.ShapeDtypeStruct((NT, PP, HEAD, 2 * BLK), f32),
            jax.ShapeDtypeStruct((PP, 3 * NT, 2 * BLK), f32),
        ],
        compiler_params=pltpu.CompilerParams(vmem_limit_bytes=VMEM),
        cost_estimate=pl.CostEstimate(
            flops=10**10, bytes_accessed=20 * 2**20, transcendentals=10**7
        ),
        name="forward" + str(group),
    )(meta, qg, kv[0], kv[-1], bias)


def backward_kernel(
    order, relative, meta, qg_ref, key_ref, value_ref, bias_ref, acc_ref, own_ref, one_ref, two_ref, three_ref,
    dkv_ref, dqa_ref, kt_ref, sum_ref, row_ref,
):
    turn_blocks(kt_ref, key_ref)
    sum_ref[...] = jnp.zeros_like(sum_ref)
    for pp in range(PP):
        parts = []
        for back, ref in enumerate((own_ref, one_ref, two_ref, three_ref)):
            stat = [ref[pp, part * NT : (part + 1) * NT, :] for part in range(3)]
            if back:
                stat = [pltpu.roll(rows, 2 * back, 0) for rows in stat]
            parts.append(stat)
        top = jnp.maximum(
            jnp.maximum(parts[0][0], parts[1][0]), jnp.maximum(parts[2][0], parts[3][0])
        )
        factors = [jnp.exp2(stat[0] - top) for stat in parts]
        total = sum(stat[1] * factor for stat, factor in zip(parts, factors))
        delta = sum(stat[2] * factor for stat, factor in zip(parts, factors))
        log_total = top + jnp.log2(total)
        row_ref[pp, :NT, :] = log_total
        row_ref[pp, NT : 2 * NT, :] = delta / total
        row_ref[pp, 2 * NT :, :] = jnp.exp2(parts[0][0] - log_total)

    def target(lt, _):
        tiles = [
            (qg_ref[lt, 0, :, cols(pp)], qg_ref[lt, 1, :, cols(pp)]) for pp in range(PP)
        ]
        rows = [(split_rows(query), split_rows(grad)) for query, grad in tiles]
        turned = [(split_cols(query), split_cols(grad)) for query, grad in tiles]
        log_totals = [row_ref[pp, pl.ds(lt, 1), :] for pp in range(PP)]
        deltas = [row_ref[pp, pl.ds(NT + lt, 1), :] for pp in range(PP)]

        def step(i, state):
            blocks = pair(meta, order[0], lt, i)
            value_blocks = pair(meta, order[1], lt, i)
            key_sums, value_sums = (pair(meta, kind, lt, i) for kind in orders(relative))
            bias = both_bias(bias_ref, *masks(meta, lt, i))
            out = []
            for pp in range(PP):
                keys = rows_of(key_ref, blocks, pp)
                values = rows_of(value_ref, value_blocks, pp)
                scores = dot(keys, turned[pp][0]) * BASE2 + bias
                probs = jnp.exp2(scores - log_totals[pp])
                grad_prob = dot(values, turned[pp][1])
                grad_score = (probs * (grad_prob - deltas[pp])).astype(bf16)
                value_part = dot(probs.astype(bf16), rows[pp][1])
                key_part = dot(grad_score, rows[pp][0])
                add_rows(sum_ref, key_sums, 0, pp, key_part)
                add_rows(sum_ref, value_sums, 1, pp, value_part)
                kt = turned_of(kt_ref, blocks, pp)
                part = wide(
                    dot(kt[:HEAD], grad_score[:, :BLK]), dot(kt[HEAD:], grad_score[:, BLK:])
                )
                out.append(state[pp] + part)
            return tuple(out)

        start = tuple(jnp.zeros((HEAD, 2 * BLK), f32) for _ in range(PP))
        state = lax.fori_loop(0, (meta[lt] + 1) // 2, step, start)
        for pp in range(PP):
            attended = acc_ref[lt, pp] * row_ref[pp, pl.ds(2 * NT + lt, 1), :]
            attended = tall(attended[:, :BLK], attended[:, BLK:])
            query_grad = tall(state[pp][:, :BLK], state[pp][:, BLK:]) * SCALE
            dqa_ref[lt, 0, :, cols(pp)] = attended.T.astype(bf16)
            dqa_ref[lt, 1, :, cols(pp)] = query_grad.T.astype(bf16)
        return 0

    lax.fori_loop(0, NT, target, 0)
    key_sum = (sum_ref[0] * SCALE).astype(bf16)
    value_sum = sum_ref[1].astype(bf16)
    if relative:
        dkv_ref[0] = key_sum
        dkv_ref[1] = value_sum
    else:
        dkv_ref[:, 0] = key_sum
        dkv_ref[:, 1] = value_sum


def backward(meta, group, relative, qg, kv, bias, acc, stats):
    shape = (2, CHIPS, 2, BLK, W) if relative else (CHIPS, 2, 2, BLK, W)
    return pl.pallas_call(
        functools.partial(backward_kernel, orders(len(kv) == 2), relative),
        grid_spec=pltpu.PrefetchScalarGridSpec(
            num_scalar_prefetch=1,
            grid=(1,),
            in_specs=[qg_spec(group)] + kv_specs(kv) + [BIAS_SPEC, ACC_SPEC] + [STAT_SPEC] * 4,
            out_specs=[pl.BlockSpec(shape, lambda p, s: (0, 0, 0, 0, 0)), OUT_SPEC],
            scratch_shapes=[
                pltpu.VMEM((CHIPS, 2, W, BLK), bf16),
                pltpu.VMEM((2, CHIPS, 2, BLK, W), f32),
                pltpu.VMEM((PP, 3 * NT, 2 * BLK), f32),
            ],
        ),
        out_shape=[
            jax.ShapeDtypeStruct(shape, bf16),
            jax.ShapeDtypeStruct((NT, 2, BLK, W), bf16),
        ],
        compiler_params=pltpu.CompilerParams(vmem_limit_bytes=VMEM),
        cost_estimate=pl.CostEstimate(
            flops=2 * 10**10, bytes_accessed=30 * 2**20, transcendentals=10**7
        ),
        name="backward" + str(group),
    )(meta, qg, kv[0], kv[-1], bias, acc, *stats)


def steps_back(rows, z):
    turned = jnp.concatenate([rows[:1], rows[3:], rows[2:3], rows[1:2]])
    return lax.dynamic_slice_in_dim(jnp.concatenate([turned, turned]), 4 - z, 4)


def tile_lists(own_adj, got_adj, side, y, x, z):
    adj = jnp.stack([own_adj, got_adj], axis=1)
    count = jnp.sum(adj, axis=2)
    first = jnp.cumsum(count, axis=0) - count + jnp.array([0, MAXT])
    adj = steps_back(adj, z).reshape(NT, NS)
    count = steps_back(count, z).reshape(NT)
    first = steps_back(first, z).reshape(NT)
    place = jnp.cumsum(adj, axis=1) - 1
    hit = (adj[:, None, :] > 0) & (place[:, None, :] == jnp.arange(NS)[None, :, None])
    index = jnp.arange(NS)
    member = index % 2 ^ side
    up, right = (y - index // 8) & 3, (x - index // 2 % 4) & 3
    lists = []
    for held in (index ^ side, 8 * up + 2 * right + member, 8 * right + 2 * up + member):
        lists.append(jnp.sum(jnp.where(hit, held[None, None, :], 0), axis=2).reshape(-1))
    return jnp.concatenate([count, first] + lists).astype(jnp.int32)


SWAP = [(0, 1), (1, 0)]


def back(array, steps, axis="z"):
    return lax.ppermute(array, axis, [(s, (s + steps) % 4) for s in range(4)])


def half(array, side):
    return lax.dynamic_slice_in_dim(array, side * HALF, HALF, array.ndim - 1)


def chip_pair(first, second, side, axis):
    both = jnp.stack([first, second])
    got = lax.ppermute(half(both, 1 - side), "k", SWAP)
    return jnp.stack([half(both, side), got], axis=axis)


def ring_gather(piece, axis):
    middle = piece.shape[0] // 2
    one, three = back(piece, 1, axis), back(piece, -1, axis)
    two = [back(one[:middle], 1, axis), back(three[middle:], -1, axis)]
    return jnp.concatenate([piece, one] + two + [three])


def ring_reduce(chunks, axis):
    middle = chunks.shape[1] // 2
    onward = back(chunks[2][:middle], 1, axis)
    backward_half = back(chunks[2][middle:], -1, axis)

    def add(mine, got):
        return (mine.astype(f32) + got.astype(f32)).astype(bf16)

    up = jnp.concatenate([add(chunks[3][:middle], onward), chunks[3][middle:]])
    down = jnp.concatenate([chunks[1][:middle], add(chunks[1][middle:], backward_half)])
    up, down = back(up, 1, axis), back(down, -1, axis)
    return chunks[0].astype(f32) + up.astype(f32) + down.astype(f32)


def reduced(part, first, second):
    rows = ring_reduce(part.reshape(4, 8, BLK, W), first).astype(bf16)
    return ring_reduce(rows.reshape(4, 2, BLK, W), second).astype(bf16)


def own_blocks(part, side):
    got = lax.ppermute(part[1], "k", SWAP)
    whole = jnp.where(
        side == 0,
        jnp.concatenate([part[0], got], axis=-1),
        jnp.concatenate([got, part[0]], axis=-1),
    )
    return whole[0], whole[1]


def z_sum(part):
    part = part.reshape(4, 2, 2, BLK, W)
    total = part[0].astype(f32)
    for steps in (1, 2, 3):
        total = total + back(part[steps], -steps).astype(f32)
    return total.astype(bf16)


def shards(node_query, node_key, node_value, grad_out, block_adjacency, edge_mask):
    side, y, x, z = (lax.axis_index(axis) for axis in ("k", "y", "x", "z"))
    plane = ("y", "x")
    kv = chip_pair(node_key, node_value, side, 1)
    late = kv[..., W:].reshape(4 * BLK, W)
    late = lax.all_gather(late, plane, axis=0, tiled=True).reshape(CHIPS, 2, 2, BLK, W)
    keys = ring_gather(ring_gather(kv[0, ..., :W], "x"), "y").reshape(CHIPS, 2, BLK, W)
    values = ring_gather(ring_gather(kv[1, ..., :W], "y"), "x").reshape(CHIPS, 2, BLK, W)
    kvs = ((keys, values), (late,))
    qg = chip_pair(node_query, grad_out, side, 0).reshape(4 * BLK, HALF)
    qg = jnp.concatenate([qg] + [back(qg, steps) for steps in (1, 2, 3)])
    qg = qg.reshape(NT, 2, BLK, HALF)
    own_adj = (block_adjacency > 0).astype(jnp.int32)
    own_bias = bias_tiles(own_adj, edge_mask)
    got_bias = lax.ppermute(own_bias, "k", SWAP)
    bias = jnp.concatenate([own_bias, got_bias, jnp.full((1, BLK, BLK), LOW, bf16)])
    got_adj = lax.ppermute(own_adj, "k", SWAP)
    meta = tile_lists(own_adj, got_adj, side, y, x, z)
    results = []
    for group in range(2):
        acc, own = forward(meta, group, qg, kvs[group], bias)
        stats = [own] + [back(own, steps) for steps in (1, 2, 3)]
        results.append(backward(meta, group, group == 1, qg, kvs[group], bias, acc, stats))
    early = lax.psum_scatter(
        results[0][0].reshape(NS * 2 * BLK, W), plane, scatter_dimension=0, tiled=True
    ).reshape(2, 2, BLK, W)
    key_late = reduced(results[1][0][0], "y", "x")
    value_late = reduced(results[1][0][1], "x", "y")
    targets = jnp.concatenate([z_sum(results[0][1]), z_sum(results[1][1])], axis=-1)
    attended, grad_query = own_blocks(targets, side)
    sources = jnp.concatenate([early, jnp.stack([key_late, value_late])], axis=-1)
    grad_key, grad_value = own_blocks(sources.transpose(1, 0, 2, 3), side)
    return (attended, grad_query, grad_key, grad_value)


def solution(mesh):
    fine = Mesh(mesh.devices.reshape(4, 4, 2, 4), ("y", "x", "k", "z"))
    row = ("y", "x", "k")
    target = P(row + ("z",), None)
    source = P(("z",) + row, None)
    tile = P(row, "z")
    return jax.shard_map(
        shards,
        mesh=fine,
        in_specs=(target, source, source, target, tile, tile),
        out_specs=(target, target, source, source),
        check_vma=False,
    )
```

```python
import functools
import math

import jax
import jax.numpy as jnp
from jax import lax
from jax.experimental import pallas as pl
from jax.experimental.pallas import tpu as pltpu
from jax.sharding import Mesh
from jax.sharding import PartitionSpec as P

D = 1024
HEADS = 16
BLK = 128
HEAD = D // HEADS
HALF = D // 2
NT = 8
NS = 32
CHIPS = NS // 2
MAXT = 32
PP = 2
W = PP * BLK
LOW = -1e30
BASE2 = math.log2(math.e) / math.sqrt(HEAD)
SCALE = 1.0 / math.sqrt(HEAD)
f32 = jnp.float32
bf16 = jnp.bfloat16
VMEM = 48 * 1024 * 1024
EMPTY = 2 * MAXT


def dot(a, b):
    return jnp.dot(a, b, preferred_element_type=f32)


def cols(pp):
    return slice(pp * BLK, (pp + 1) * BLK)


def wide(first, second):
    return jnp.concatenate([first, second], axis=1)


def tall(first, second):
    return jnp.concatenate([first, second], axis=0)


def split_rows(tile):
    lane = lax.broadcasted_iota(jnp.int32, tile.shape, 1)
    zero = jnp.zeros_like(tile)
    return tall(jnp.where(lane < HEAD, tile, zero), jnp.where(lane >= HEAD, tile, zero))


def split_cols(tile):
    turned = tile.T
    zero = jnp.zeros((HEAD, BLK), tile.dtype)
    return wide(tall(turned[:HEAD], zero), tall(zero, turned[HEAD:]))


def bias_kernel(adj, mask_ref, out_ref, slot):
    row = pl.program_id(0)

    @pl.when(row == 0)
    def _():
        slot[0] = 0
        out_ref[...] = jnp.full(out_ref.shape, LOW, bf16)

    for s in range(NS):

        @pl.when(adj[row, s] > 0)
        def _():
            edge = mask_ref[:, s * BLK : (s + 1) * BLK]
            tile = jnp.where(edge > 0, 0.0, LOW).astype(f32)
            out_ref[jnp.minimum(slot[0], MAXT - 1)] = tile.T.astype(bf16)
            slot[0] = slot[0] + 1


def bias_tiles(adjacency, edge_mask):
    return pl.pallas_call(
        bias_kernel,
        grid_spec=pltpu.PrefetchScalarGridSpec(
            num_scalar_prefetch=1,
            grid=(4,),
            in_specs=[pl.BlockSpec((BLK, NS * BLK), lambda i, s: (i, 0))],
            out_specs=pl.BlockSpec((MAXT, BLK, BLK), lambda i, s: (0, 0, 0)),
            scratch_shapes=[pltpu.SMEM((1,), jnp.int32)],
        ),
        out_shape=jax.ShapeDtypeStruct((MAXT, BLK, BLK), bf16),
        compiler_params=pltpu.CompilerParams(vmem_limit_bytes=VMEM),
        cost_estimate=pl.CostEstimate(flops=0, bytes_accessed=30 * 2**20, transcendentals=0),
        name="bias_tiles",
    )(adjacency, edge_mask)


ABSOLUTE, RELATIVE_KEY, RELATIVE_VALUE = range(3)


def block(meta, order, lt, slot):
    index = meta[2 * NT + (order * NT + lt) * NS + slot]
    return index // 2, index % 2


def pair(meta, order, lt, i):
    return block(meta, order, lt, 2 * i), block(meta, order, lt, 2 * i + 1)


def masks(meta, lt, i):
    first = meta[NT + lt] + 2 * i
    return first, jnp.where(2 * i + 1 < meta[lt], first + 1, EMPTY)


def orders(relative):
    return (RELATIVE_KEY, RELATIVE_VALUE) if relative else (ABSOLUTE, ABSOLUTE)


def both_bias(bias_ref, b0, b1):
    bias = tall(bias_ref[b0], bias_ref[b1]).astype(f32)
    return wide(bias, bias)


def turn_blocks(turned_ref, ref):
    def turn(chip, _):
        for member in range(2):
            for pp in range(PP):
                turned_ref[chip, member, cols(pp), :] = ref[chip, member, :, cols(pp)].T
        return 0

    lax.fori_loop(0, CHIPS, turn, 0)


def rows_of(ref, blocks, pp):
    (c0, m0), (c1, m1) = blocks
    return tall(ref[c0, m0, :, cols(pp)], ref[c1, m1, :, cols(pp)])


def turned_of(ref, blocks, pp):
    (c0, m0), (c1, m1) = blocks
    return wide(ref[c0, m0, cols(pp), :], ref[c1, m1, cols(pp), :])


def add_rows(ref, blocks, kind, pp, part):
    for (chip, member), rows in zip(blocks, (part[:BLK], part[BLK:])):
        ref[kind, chip, member, :, cols(pp)] += rows


def forward_kernel(
    meta, qg_ref, key_ref, value_ref, bias_ref, acc_ref, stat_ref, vt_ref, score_ref
):
    turn_blocks(vt_ref, value_ref)

    def target(lt, _):
        queries = [split_cols(qg_ref[lt, 0, :, cols(pp)]) for pp in range(PP)]
        turns = (meta[lt] + 1) // 2

        def score_step(i, tops):
            blocks = pair(meta, ABSOLUTE, lt, i)
            bias = both_bias(bias_ref, *masks(meta, lt, i))
            out = []
            for pp in range(PP):
                keys = rows_of(key_ref, blocks, pp)
                scores = dot(keys, queries[pp]) * BASE2 + bias
                score_ref[i, pp] = scores
                top = jnp.max(scores.reshape(-1, 8, 2 * BLK), axis=0)
                out.append(jnp.maximum(tops[pp], top))
            return tuple(out)

        tops = lax.fori_loop(
            0, turns, score_step, tuple(jnp.full((8, 2 * BLK), LOW, f32) for _ in range(PP))
        )
        tops = [jnp.max(top, axis=0, keepdims=True) for top in tops]

        def weight_step(i, state):
            blocks = pair(meta, ABSOLUTE, lt, i)
            out = []
            for pp in range(PP):
                total, acc = state[pp]
                weights = jnp.exp2(score_ref[i, pp] - tops[pp])
                total = total + jnp.sum(weights.reshape(-1, 8, 2 * BLK), axis=0)
                low = weights.astype(bf16)
                vt = turned_of(vt_ref, blocks, pp)
                part = wide(dot(vt[:HEAD], low[:, :BLK]), dot(vt[HEAD:], low[:, BLK:]))
                out.append((total, acc + part))
            return tuple(out)

        start = tuple(
            (jnp.zeros((8, 2 * BLK), f32), jnp.zeros((HEAD, 2 * BLK), f32)) for _ in range(PP)
        )
        state = lax.fori_loop(0, turns, weight_step, start)
        for pp in range(PP):
            total, acc = state[pp]
            grad = qg_ref[lt, 1, :, cols(pp)].T.astype(f32)
            grad = wide(grad[:HEAD], grad[HEAD:])
            acc_ref[lt, pp] = acc
            stat_ref[pp, pl.ds(lt, 1), :] = tops[pp]
            stat_ref[pp, pl.ds(NT + lt, 1), :] = jnp.sum(total, axis=0, keepdims=True)
            stat_ref[pp, pl.ds(2 * NT + lt, 1), :] = jnp.sum(acc * grad, axis=0, keepdims=True)
        return 0

    lax.fori_loop(0, NT, target, 0)


BIAS_SPEC = pl.BlockSpec((EMPTY + 1, BLK, BLK), lambda p, s: (0, 0, 0))
ACC_SPEC = pl.BlockSpec((NT, PP, HEAD, 2 * BLK), lambda p, s: (0, 0, 0, 0))
STAT_SPEC = pl.BlockSpec((PP, 3 * NT, 2 * BLK), lambda p, s: (0, 0, 0))
OUT_SPEC = pl.BlockSpec((NT, 2, BLK, W), lambda p, s: (0, 0, 0, 0))


def qg_spec(group):
    return pl.BlockSpec((NT, 2, BLK, W), lambda p, s: (0, 0, 0, group))


def kind_spec(kind):
    return pl.BlockSpec((CHIPS, None, 2, BLK, W), lambda p, s: (0, kind, 0, 0, 0))


def forward(meta, group, qg, kv, bias):
    return pl.pallas_call(
        forward_kernel,
        grid_spec=pltpu.PrefetchScalarGridSpec(
            num_scalar_prefetch=1,
            grid=(1,),
            in_specs=[qg_spec(group), kind_spec(0), kind_spec(1), BIAS_SPEC],
            out_specs=[ACC_SPEC, STAT_SPEC],
            scratch_shapes=[
                pltpu.VMEM((CHIPS, 2, W, BLK), bf16),
                pltpu.VMEM((NS // 2, PP, 2 * BLK, 2 * BLK), f32),
            ],
        ),
        out_shape=[
            jax.ShapeDtypeStruct((NT, PP, HEAD, 2 * BLK), f32),
            jax.ShapeDtypeStruct((PP, 3 * NT, 2 * BLK), f32),
        ],
        compiler_params=pltpu.CompilerParams(vmem_limit_bytes=VMEM),
        cost_estimate=pl.CostEstimate(
            flops=10**10, bytes_accessed=20 * 2**20, transcendentals=10**7
        ),
        name="forward" + str(group),
    )(meta, qg, kv, kv, bias)


def backward_kernel(
    relative, meta, qg_ref, key_ref, value_ref, bias_ref, acc_ref, own_ref, one_ref, two_ref, three_ref,
    dkv_ref, dqa_ref, kt_ref, sum_ref, row_ref,
):
    turn_blocks(kt_ref, key_ref)
    sum_ref[...] = jnp.zeros_like(sum_ref)
    for pp in range(PP):
        parts = []
        for back, ref in enumerate((own_ref, one_ref, two_ref, three_ref)):
            stat = [ref[pp, part * NT : (part + 1) * NT, :] for part in range(3)]
            if back:
                stat = [pltpu.roll(rows, 2 * back, 0) for rows in stat]
            parts.append(stat)
        top = jnp.maximum(
            jnp.maximum(parts[0][0], parts[1][0]), jnp.maximum(parts[2][0], parts[3][0])
        )
        factors = [jnp.exp2(stat[0] - top) for stat in parts]
        total = sum(stat[1] * factor for stat, factor in zip(parts, factors))
        delta = sum(stat[2] * factor for stat, factor in zip(parts, factors))
        log_total = top + jnp.log2(total)
        row_ref[pp, :NT, :] = log_total
        row_ref[pp, NT : 2 * NT, :] = delta / total
        row_ref[pp, 2 * NT :, :] = jnp.exp2(parts[0][0] - log_total)

    def target(lt, _):
        tiles = [
            (qg_ref[lt, 0, :, cols(pp)], qg_ref[lt, 1, :, cols(pp)]) for pp in range(PP)
        ]
        rows = [(split_rows(query), split_rows(grad)) for query, grad in tiles]
        turned = [(split_cols(query), split_cols(grad)) for query, grad in tiles]
        log_totals = [row_ref[pp, pl.ds(lt, 1), :] for pp in range(PP)]
        deltas = [row_ref[pp, pl.ds(NT + lt, 1), :] for pp in range(PP)]

        def step(i, state):
            blocks = pair(meta, ABSOLUTE, lt, i)
            key_sums, value_sums = (pair(meta, kind, lt, i) for kind in orders(relative))
            bias = both_bias(bias_ref, *masks(meta, lt, i))
            out = []
            for pp in range(PP):
                keys = rows_of(key_ref, blocks, pp)
                values = rows_of(value_ref, blocks, pp)
                scores = dot(keys, turned[pp][0]) * BASE2 + bias
                probs = jnp.exp2(scores - log_totals[pp])
                grad_prob = dot(values, turned[pp][1])
                grad_score = (probs * (grad_prob - deltas[pp])).astype(bf16)
                value_part = dot(probs.astype(bf16), rows[pp][1])
                key_part = dot(grad_score, rows[pp][0])
                add_rows(sum_ref, key_sums, 0, pp, key_part)
                add_rows(sum_ref, value_sums, 1, pp, value_part)
                kt = turned_of(kt_ref, blocks, pp)
                part = wide(
                    dot(kt[:HEAD], grad_score[:, :BLK]), dot(kt[HEAD:], grad_score[:, BLK:])
                )
                out.append(state[pp] + part)
            return tuple(out)

        start = tuple(jnp.zeros((HEAD, 2 * BLK), f32) for _ in range(PP))
        state = lax.fori_loop(0, (meta[lt] + 1) // 2, step, start)
        for pp in range(PP):
            attended = acc_ref[lt, pp] * row_ref[pp, pl.ds(2 * NT + lt, 1), :]
            attended = tall(attended[:, :BLK], attended[:, BLK:])
            query_grad = tall(state[pp][:, :BLK], state[pp][:, BLK:]) * SCALE
            dqa_ref[lt, 0, :, cols(pp)] = attended.T.astype(bf16)
            dqa_ref[lt, 1, :, cols(pp)] = query_grad.T.astype(bf16)
        return 0

    lax.fori_loop(0, NT, target, 0)
    key_sum = (sum_ref[0] * SCALE).astype(bf16)
    value_sum = sum_ref[1].astype(bf16)
    if relative:
        dkv_ref[0] = key_sum
        dkv_ref[1] = value_sum
    else:
        dkv_ref[:, 0] = key_sum
        dkv_ref[:, 1] = value_sum


def backward(meta, group, relative, qg, kv, bias, acc, stats):
    shape = (2, CHIPS, 2, BLK, W) if relative else (CHIPS, 2, 2, BLK, W)
    return pl.pallas_call(
        functools.partial(backward_kernel, relative),
        grid_spec=pltpu.PrefetchScalarGridSpec(
            num_scalar_prefetch=1,
            grid=(1,),
            in_specs=[qg_spec(group), kind_spec(0), kind_spec(1), BIAS_SPEC, ACC_SPEC] + [STAT_SPEC] * 4,
            out_specs=[pl.BlockSpec(shape, lambda p, s: (0, 0, 0, 0, 0)), OUT_SPEC],
            scratch_shapes=[
                pltpu.VMEM((CHIPS, 2, W, BLK), bf16),
                pltpu.VMEM((2, CHIPS, 2, BLK, W), f32),
                pltpu.VMEM((PP, 3 * NT, 2 * BLK), f32),
            ],
        ),
        out_shape=[
            jax.ShapeDtypeStruct(shape, bf16),
            jax.ShapeDtypeStruct((NT, 2, BLK, W), bf16),
        ],
        compiler_params=pltpu.CompilerParams(vmem_limit_bytes=VMEM),
        cost_estimate=pl.CostEstimate(
            flops=2 * 10**10, bytes_accessed=30 * 2**20, transcendentals=10**7
        ),
        name="backward" + str(group),
    )(meta, qg, kv, kv, bias, acc, *stats)


def steps_back(rows, z):
    turned = jnp.concatenate([rows[:1], rows[3:], rows[2:3], rows[1:2]])
    return lax.dynamic_slice_in_dim(jnp.concatenate([turned, turned]), 4 - z, 4)


def tile_lists(own_adj, got_adj, side, y, x, z):
    adj = jnp.stack([own_adj, got_adj], axis=1)
    count = jnp.sum(adj, axis=2)
    first = jnp.cumsum(count, axis=0) - count + jnp.array([0, MAXT])
    adj = steps_back(adj, z).reshape(NT, NS)
    count = steps_back(count, z).reshape(NT)
    first = steps_back(first, z).reshape(NT)
    place = jnp.cumsum(adj, axis=1) - 1
    hit = (adj[:, None, :] > 0) & (place[:, None, :] == jnp.arange(NS)[None, :, None])
    index = jnp.arange(NS)
    member = index % 2 ^ side
    up, right = (y - index // 8) & 3, (x - index // 2 % 4) & 3
    lists = []
    for held in (index ^ side, 8 * up + 2 * right + member, 8 * right + 2 * up + member):
        lists.append(jnp.sum(jnp.where(hit, held[None, None, :], 0), axis=2).reshape(-1))
    return jnp.concatenate([count, first] + lists).astype(jnp.int32)


SWAP = [(0, 1), (1, 0)]


def back(array, steps, axis="z"):
    return lax.ppermute(array, axis, [(s, (s + steps) % 4) for s in range(4)])


def half(array, side):
    return lax.dynamic_slice_in_dim(array, side * HALF, HALF, array.ndim - 1)


def chip_pair(first, second, side, axis):
    both = jnp.stack([first, second])
    got = lax.ppermute(half(both, 1 - side), "k", SWAP)
    return jnp.stack([half(both, side), got], axis=axis)


def ring_reduce(chunks, axis):
    middle = chunks.shape[1] // 2
    onward = back(chunks[2][:middle], 1, axis)
    backward_half = back(chunks[2][middle:], -1, axis)

    def add(mine, got):
        return (mine.astype(f32) + got.astype(f32)).astype(bf16)

    up = jnp.concatenate([add(chunks[3][:middle], onward), chunks[3][middle:]])
    down = jnp.concatenate([chunks[1][:middle], add(chunks[1][middle:], backward_half)])
    up, down = back(up, 1, axis), back(down, -1, axis)
    return chunks[0].astype(f32) + up.astype(f32) + down.astype(f32)


def reduced(part, first, second):
    rows = ring_reduce(part.reshape(4, 8, BLK, W), first).astype(bf16)
    return ring_reduce(rows.reshape(4, 2, BLK, W), second).astype(bf16)


def own_blocks(part, side):
    got = lax.ppermute(part[1], "k", SWAP)
    whole = jnp.where(
        side == 0,
        jnp.concatenate([part[0], got], axis=-1),
        jnp.concatenate([got, part[0]], axis=-1),
    )
    return whole[0], whole[1]


def z_sum(part):
    part = part.reshape(4, 2, 2, BLK, W)
    total = part[0].astype(f32)
    for steps in (1, 2, 3):
        total = total + back(part[steps], -steps).astype(f32)
    return total.astype(bf16)


def shards(node_query, node_key, node_value, grad_out, block_adjacency, edge_mask):
    side, y, x, z = (lax.axis_index(axis) for axis in ("k", "y", "x", "z"))
    plane = ("y", "x")
    kv = chip_pair(node_key, node_value, side, 1)
    kvs = []
    for group in range(2):
        part = kv[..., group * W : (group + 1) * W].reshape(4 * BLK, W)
        whole = lax.all_gather(part, plane, axis=0, tiled=True)
        kvs.append(whole.reshape(CHIPS, 2, 2, BLK, W))
    qg = chip_pair(node_query, grad_out, side, 0).reshape(4 * BLK, HALF)
    qg = jnp.concatenate([qg] + [back(qg, steps) for steps in (1, 2, 3)])
    qg = qg.reshape(NT, 2, BLK, HALF)
    own_adj = (block_adjacency > 0).astype(jnp.int32)
    own_bias = bias_tiles(own_adj, edge_mask)
    got_bias = lax.ppermute(own_bias, "k", SWAP)
    bias = jnp.concatenate([own_bias, got_bias, jnp.full((1, BLK, BLK), LOW, bf16)])
    got_adj = lax.ppermute(own_adj, "k", SWAP)
    meta = tile_lists(own_adj, got_adj, side, y, x, z)
    results = []
    for group in range(2):
        acc, own = forward(meta, group, qg, kvs[group], bias)
        stats = [own] + [back(own, steps) for steps in (1, 2, 3)]
        results.append(backward(meta, group, group == 1, qg, kvs[group], bias, acc, stats))
    early = lax.psum_scatter(
        results[0][0].reshape(NS * 2 * BLK, W), plane, scatter_dimension=0, tiled=True
    ).reshape(2, 2, BLK, W)
    key_late = reduced(results[1][0][0], "y", "x")
    value_late = reduced(results[1][0][1], "x", "y")
    targets = jnp.concatenate([z_sum(results[0][1]), z_sum(results[1][1])], axis=-1)
    attended, grad_query = own_blocks(targets, side)
    sources = jnp.concatenate([early, jnp.stack([key_late, value_late])], axis=-1)
    grad_key, grad_value = own_blocks(sources.transpose(1, 0, 2, 3), side)
    return (attended, grad_query, grad_key, grad_value)


def solution(mesh):
    fine = Mesh(mesh.devices.reshape(4, 4, 2, 4), ("y", "x", "k", "z"))
    row = ("y", "x", "k")
    target = P(row + ("z",), None)
    source = P(("z",) + row, None)
    tile = P(row, "z")
    return jax.shard_map(
        shards,
        mesh=fine,
        in_specs=(target, source, source, target, tile, tile),
        out_specs=(target, target, source, source),
        check_vma=False,
    )
```

```python
import functools
import math

import jax
import jax.numpy as jnp
from jax import lax
from jax.experimental import pallas as pl
from jax.experimental.pallas import tpu as pltpu
from jax.sharding import Mesh
from jax.sharding import PartitionSpec as P

D = 1024
HEADS = 16
BLK = 128
HEAD = D // HEADS
HALF = D // 2
NT = 8
NS = 32
CHIPS = NS // 2
MAXT = 32
GROUPS = (3, 1)
LOW = -1e30
BASE2 = math.log2(math.e) / math.sqrt(HEAD)
SCALE = 1.0 / math.sqrt(HEAD)
f32 = jnp.float32
bf16 = jnp.bfloat16
VMEM = 56 * 1024 * 1024
EMPTY = 2 * MAXT


def dot(a, b):
    return jnp.dot(a, b, preferred_element_type=f32)


def cols(pp):
    return slice(pp * BLK, (pp + 1) * BLK)


def wide(first, second):
    return jnp.concatenate([first, second], axis=1)


def tall(first, second):
    return jnp.concatenate([first, second], axis=0)


def split_rows(tile):
    lane = lax.broadcasted_iota(jnp.int32, tile.shape, 1)
    zero = jnp.zeros_like(tile)
    return tall(jnp.where(lane < HEAD, tile, zero), jnp.where(lane >= HEAD, tile, zero))


def split_cols(tile):
    turned = tile.T
    zero = jnp.zeros((HEAD, BLK), tile.dtype)
    return wide(tall(turned[:HEAD], zero), tall(zero, turned[HEAD:]))


def bias_kernel(adj, mask_ref, out_ref, slot):
    row = pl.program_id(0)

    @pl.when(row == 0)
    def _():
        slot[0] = 0
        out_ref[...] = jnp.full(out_ref.shape, LOW, bf16)

    for s in range(NS):

        @pl.when(adj[row, s] > 0)
        def _():
            edge = mask_ref[:, s * BLK : (s + 1) * BLK]
            tile = jnp.where(edge > 0, 0.0, LOW).astype(f32)
            out_ref[jnp.minimum(slot[0], MAXT - 1)] = tile.T.astype(bf16)
            slot[0] = slot[0] + 1


def bias_tiles(adjacency, edge_mask):
    return pl.pallas_call(
        bias_kernel,
        grid_spec=pltpu.PrefetchScalarGridSpec(
            num_scalar_prefetch=1,
            grid=(4,),
            in_specs=[pl.BlockSpec((BLK, NS * BLK), lambda i, s: (i, 0))],
            out_specs=pl.BlockSpec((MAXT, BLK, BLK), lambda i, s: (0, 0, 0)),
            scratch_shapes=[pltpu.SMEM((1,), jnp.int32)],
        ),
        out_shape=jax.ShapeDtypeStruct((MAXT, BLK, BLK), bf16),
        compiler_params=pltpu.CompilerParams(vmem_limit_bytes=VMEM),
        cost_estimate=pl.CostEstimate(flops=0, bytes_accessed=30 * 2**20, transcendentals=0),
        name="bias_tiles",
    )(adjacency, edge_mask)


def block(meta, lt, slot):
    index = meta[2 * NT + lt * NS + slot]
    return index // 2, index % 2


def tiles(meta, lt, i):
    first = meta[NT + lt] + 2 * i
    second = jnp.where(2 * i + 1 < meta[lt], first + 1, EMPTY)
    return (block(meta, lt, 2 * i), block(meta, lt, 2 * i + 1)), (first, second)


def both_bias(bias_ref, places):
    bias = tall(bias_ref[places[0]], bias_ref[places[1]]).astype(f32)
    return wide(bias, bias)


def run(turns, step, state):
    state = lax.fori_loop(0, turns // 2, lambda j, held: step(2 * j + 1, step(2 * j, held)), state)
    return lax.fori_loop(0, turns % 2, lambda _, held: step(turns - 1, held), state)


def turn_blocks(pairs, turned_ref, ref):
    def turn(i, _):
        for j in range(4):
            for member in range(2):
                for pp in range(pairs):
                    chip = 4 * i + j
                    turned_ref[chip, member, cols(pp), :] = ref[chip, member, :, cols(pp)].T
        return 0

    lax.fori_loop(0, CHIPS // 4, turn, 0)


def rows_of(ref, blocks, pp):
    (c0, m0), (c1, m1) = blocks
    return tall(ref[c0, m0, :, cols(pp)], ref[c1, m1, :, cols(pp)])


def turned_of(ref, blocks, pp):
    (c0, m0), (c1, m1) = blocks
    return wide(ref[c0, m0, cols(pp), :], ref[c1, m1, cols(pp), :])


def add_rows(ref, blocks, kind, pp, part):
    for (chip, member), rows in zip(blocks, (part[:BLK], part[BLK:])):
        ref[kind, chip, member, :, cols(pp)] += rows


def forward_kernel(
    pairs, meta, qg_ref, key_ref, value_ref, bias_ref, acc_ref, stat_ref, vt_ref, query_ref, score_ref
):
    turn_blocks(pairs, vt_ref, value_ref)
    for lt in range(NT):
        for pp in range(pairs):
            query_ref[lt, pp] = split_cols(qg_ref[lt, 0, :, cols(pp)])

    def target(lt, _):
        turns = (meta[lt] + 1) // 2

        def score_step(i, tops):
            blocks, places = tiles(meta, lt, i)
            bias = both_bias(bias_ref, places)
            out = []
            for pp in range(pairs):
                keys = rows_of(key_ref, blocks, pp)
                scores = dot(keys, query_ref[lt, pp]) * BASE2 + bias
                score_ref[i, pp] = scores
                top = jnp.max(scores.reshape(-1, 8, 2 * BLK), axis=0)
                out.append(jnp.maximum(tops[pp], top))
            return tuple(out)

        tops = run(turns, score_step, tuple(jnp.full((8, 2 * BLK), LOW, f32) for _ in range(pairs)))
        tops = [jnp.max(top, axis=0, keepdims=True) for top in tops]

        def weight_step(i, state):
            blocks, _ = tiles(meta, lt, i)
            out = []
            for pp in range(pairs):
                total, acc = state[pp]
                weights = jnp.exp2(score_ref[i, pp] - tops[pp])
                total = total + jnp.sum(weights.reshape(-1, 8, 2 * BLK), axis=0)
                low = weights.astype(bf16)
                vt = turned_of(vt_ref, blocks, pp)
                part = wide(dot(vt[:HEAD], low[:, :BLK]), dot(vt[HEAD:], low[:, BLK:]))
                out.append((total, acc + part))
            return tuple(out)

        start = tuple(
            (jnp.zeros((8, 2 * BLK), f32), jnp.zeros((HEAD, 2 * BLK), f32)) for _ in range(pairs)
        )
        state = run(turns, weight_step, start)
        for pp in range(pairs):
            total, acc = state[pp]
            acc_ref[lt, pp] = acc
            stat_ref[pp, pl.ds(lt, 1), :] = tops[pp]
            stat_ref[pp, pl.ds(NT + lt, 1), :] = jnp.sum(total, axis=0, keepdims=True)
        return 0

    lax.fori_loop(0, NT, target, 0)
    for pp in range(pairs):
        deltas = []
        for lt in range(NT):
            grad = qg_ref[lt, 1, :, cols(pp)].T.astype(f32)
            grad = wide(grad[:HEAD], grad[HEAD:])
            deltas.append(jnp.sum(acc_ref[lt, pp] * grad, axis=0, keepdims=True))
        stat_ref[pp, 2 * NT :, :] = jnp.concatenate(deltas)


def spec(shape, *index):
    return pl.BlockSpec(shape, lambda p, s: index, pipeline_mode=pl.Buffered(1))


def specs(pairs, start):
    width = pairs * BLK
    return (
        spec((NT, 2, BLK, width), 0, 0, 0, start // pairs),
        [spec((CHIPS, None, 2, BLK, width), 0, kind, 0, 0, 0) for kind in range(2)],
        spec((EMPTY + 1, BLK, BLK), 0, 0, 0),
        spec((NT, pairs, HEAD, 2 * BLK), 0, 0, 0, 0),
        spec((pairs, 3 * NT, 2 * BLK), 0, 0, 0),
    )


def forward(meta, pairs, start, qg, kv, bias):
    qg_spec, kv_specs, bias_spec, acc_spec, stat_spec = specs(pairs, start)
    return pl.pallas_call(
        functools.partial(forward_kernel, pairs),
        grid_spec=pltpu.PrefetchScalarGridSpec(
            num_scalar_prefetch=1,
            grid=(1,),
            in_specs=[qg_spec] + kv_specs + [bias_spec],
            out_specs=[acc_spec, stat_spec],
            scratch_shapes=[
                pltpu.VMEM((CHIPS, 2, pairs * BLK, BLK), bf16),
                pltpu.VMEM((NT, pairs, BLK, 2 * BLK), bf16),
                pltpu.VMEM((NS // 2, pairs, 2 * BLK, 2 * BLK), f32),
            ],
        ),
        out_shape=[
            jax.ShapeDtypeStruct((NT, pairs, HEAD, 2 * BLK), f32),
            jax.ShapeDtypeStruct((pairs, 3 * NT, 2 * BLK), f32),
        ],
        compiler_params=pltpu.CompilerParams(vmem_limit_bytes=VMEM),
        cost_estimate=pl.CostEstimate(
            flops=10**10, bytes_accessed=20 * 2**20, transcendentals=10**7
        ),
        name="forward" + str(start),
    )(meta, qg, kv, kv, bias)


def backward_kernel(
    pairs, meta, qg_ref, key_ref, value_ref, bias_ref, acc_ref, own_ref, one_ref, two_ref, three_ref,
    dkv_ref, dqa_ref, kt_ref, turned_ref, dq_ref, sum_ref, row_ref,
):
    turn_blocks(pairs, kt_ref, key_ref)
    for lt in range(NT):
        for pp in range(pairs):
            for kind in range(2):
                turned_ref[lt, pp, kind] = split_cols(qg_ref[lt, kind, :, cols(pp)])
    sum_ref[...] = jnp.zeros_like(sum_ref)
    for pp in range(pairs):
        parts = []
        for back, ref in enumerate((own_ref, one_ref, two_ref, three_ref)):
            stat = [ref[pp, part * NT : (part + 1) * NT, :] for part in range(3)]
            if back:
                stat = [pltpu.roll(rows, 2 * back, 0) for rows in stat]
            parts.append(stat)
        top = jnp.maximum(
            jnp.maximum(parts[0][0], parts[1][0]), jnp.maximum(parts[2][0], parts[3][0])
        )
        factors = [jnp.exp2(stat[0] - top) for stat in parts]
        total = sum(stat[1] * factor for stat, factor in zip(parts, factors))
        delta = sum(stat[2] * factor for stat, factor in zip(parts, factors))
        log_total = top + jnp.log2(total)
        row_ref[pp, :NT, :] = log_total
        row_ref[pp, NT : 2 * NT, :] = delta / total
        row_ref[pp, 2 * NT :, :] = jnp.exp2(parts[0][0] - log_total)

    def target(lt, _):
        rows = [
            [split_rows(qg_ref[lt, kind, :, cols(pp)]) for kind in range(2)] for pp in range(pairs)
        ]
        log_totals = [row_ref[pp, pl.ds(lt, 1), :] for pp in range(pairs)]
        deltas = [row_ref[pp, pl.ds(NT + lt, 1), :] for pp in range(pairs)]

        def step(i, state):
            blocks, places = tiles(meta, lt, i)
            bias = both_bias(bias_ref, places)
            out = []
            for pp in range(pairs):
                keys = rows_of(key_ref, blocks, pp)
                values = rows_of(value_ref, blocks, pp)
                scores = dot(keys, turned_ref[lt, pp, 0]) * BASE2 + bias
                probs = jnp.exp2(scores - log_totals[pp])
                grad_prob = dot(values, turned_ref[lt, pp, 1])
                grad_score = (probs * (grad_prob - deltas[pp])).astype(bf16)
                value_part = dot(probs.astype(bf16), rows[pp][1])
                key_part = dot(grad_score, rows[pp][0])
                add_rows(sum_ref, blocks, 0, pp, key_part)
                add_rows(sum_ref, blocks, 1, pp, value_part)
                kt = turned_of(kt_ref, blocks, pp)
                part = wide(
                    dot(kt[:HEAD], grad_score[:, :BLK]), dot(kt[HEAD:], grad_score[:, BLK:])
                )
                out.append(state[pp] + part)
            return tuple(out)

        start = tuple(jnp.zeros((HEAD, 2 * BLK), f32) for _ in range(pairs))
        state = run((meta[lt] + 1) // 2, step, start)
        for pp in range(pairs):
            dq_ref[lt, pp] = state[pp] * SCALE
        return 0

    lax.fori_loop(0, NT, target, 0)

    def finish(i, _):
        for lt in (2 * i, 2 * i + 1):
            for pp in range(pairs):
                attended = acc_ref[lt, pp] * row_ref[pp, pl.ds(2 * NT + lt, 1), :]
                for kind, pair in enumerate((attended, dq_ref[lt, pp])):
                    pair = tall(pair[:, :BLK], pair[:, BLK:])
                    dqa_ref[lt, kind, :, cols(pp)] = pair.T.astype(bf16)
        return 0

    lax.fori_loop(0, NT // 2, finish, 0)
    dkv_ref[:, 0] = (sum_ref[0] * SCALE).astype(bf16)
    dkv_ref[:, 1] = sum_ref[1].astype(bf16)


def backward(meta, pairs, start, qg, kv, bias, acc, stats):
    qg_spec, kv_specs, bias_spec, acc_spec, stat_spec = specs(pairs, start)
    width = pairs * BLK
    return pl.pallas_call(
        functools.partial(backward_kernel, pairs),
        grid_spec=pltpu.PrefetchScalarGridSpec(
            num_scalar_prefetch=1,
            grid=(1,),
            in_specs=[qg_spec] + kv_specs + [bias_spec, acc_spec] + [stat_spec] * 4,
            out_specs=[
                spec((CHIPS, 2, 2, BLK, width), 0, 0, 0, 0, 0),
                spec((NT, 2, BLK, width), 0, 0, 0, 0),
            ],
            scratch_shapes=[
                pltpu.VMEM((CHIPS, 2, width, BLK), bf16),
                pltpu.VMEM((NT, pairs, 2, BLK, 2 * BLK), bf16),
                pltpu.VMEM((NT, pairs, HEAD, 2 * BLK), f32),
                pltpu.VMEM((2, CHIPS, 2, BLK, width), f32),
                pltpu.VMEM((pairs, 3 * NT, 2 * BLK), f32),
            ],
        ),
        out_shape=[
            jax.ShapeDtypeStruct((CHIPS, 2, 2, BLK, width), bf16),
            jax.ShapeDtypeStruct((NT, 2, BLK, width), bf16),
        ],
        compiler_params=pltpu.CompilerParams(vmem_limit_bytes=VMEM),
        cost_estimate=pl.CostEstimate(
            flops=2 * 10**10, bytes_accessed=30 * 2**20, transcendentals=10**7
        ),
        name="backward" + str(start),
    )(meta, qg, kv, kv, bias, acc, *stats)


def steps_back(rows, z):
    turned = jnp.concatenate([rows[:1], rows[3:], rows[2:3], rows[1:2]])
    return lax.dynamic_slice_in_dim(jnp.concatenate([turned, turned]), 4 - z, 4)


def tile_lists(own_adj, got_adj, side, z):
    adj = jnp.stack([own_adj, got_adj], axis=1)
    count = jnp.sum(adj, axis=2)
    first = jnp.cumsum(count, axis=0) - count + jnp.array([0, MAXT])
    adj = steps_back(adj, z).reshape(NT, NS)
    count = steps_back(count, z).reshape(NT)
    first = steps_back(first, z).reshape(NT)
    place = jnp.cumsum(adj, axis=1) - 1
    hit = (adj[:, None, :] > 0) & (place[:, None, :] == jnp.arange(NS)[None, :, None])
    held = jnp.arange(NS) ^ side
    source = jnp.sum(jnp.where(hit, held[None, None, :], 0), axis=2)
    return jnp.concatenate([count, first, source.reshape(-1)]).astype(jnp.int32)


SWAP = [(0, 1), (1, 0)]


def back(array, steps):
    return lax.ppermute(array, "z", [(s, (s + steps) % 4) for s in range(4)])


def half(array, side):
    return lax.dynamic_slice_in_dim(array, side * HALF, HALF, array.ndim - 1)


def chip_pair(first, second, side, axis):
    both = jnp.stack([first, second])
    got = lax.ppermute(half(both, 1 - side), "k", SWAP)
    return jnp.stack([half(both, side), got], axis=axis)


def own_blocks(part, side):
    got = lax.ppermute(part[1], "k", SWAP)
    whole = jnp.where(
        side == 0,
        jnp.concatenate([part[0], got], axis=-1),
        jnp.concatenate([got, part[0]], axis=-1),
    )
    return whole[0], whole[1]


def z_sum(part):
    part = part.reshape(4, 2, 2, BLK, -1)
    total = part[0].astype(f32)
    for steps in (1, 2, 3):
        total = total + back(part[steps], -steps).astype(f32)
    return total.astype(bf16)


def shards(node_query, node_key, node_value, grad_out, block_adjacency, edge_mask):
    side, z = lax.axis_index("k"), lax.axis_index("z")
    plane = ("y", "x")
    kv = chip_pair(node_key, node_value, side, 1)
    groups, start = [], 0
    for pairs in GROUPS:
        width = pairs * BLK
        part = kv[..., start * BLK : start * BLK + width].reshape(4 * BLK, width)
        whole = lax.all_gather(part, plane, axis=0, tiled=True)
        groups.append((pairs, start, whole.reshape(CHIPS, 2, 2, BLK, width)))
        start += pairs
    qg = chip_pair(node_query, grad_out, side, 0).reshape(4 * BLK, HALF)
    qg = jnp.concatenate([qg] + [back(qg, steps) for steps in (1, 2, 3)])
    qg = qg.reshape(NT, 2, BLK, HALF)
    own_adj = (block_adjacency > 0).astype(jnp.int32)
    own_bias = bias_tiles(own_adj, edge_mask)
    got_bias = lax.ppermute(own_bias, "k", SWAP)
    bias = jnp.concatenate([own_bias, got_bias, jnp.full((1, BLK, BLK), LOW, bf16)])
    got_adj = lax.ppermute(own_adj, "k", SWAP)
    meta = tile_lists(own_adj, got_adj, side, z)
    sources, targets = [], []
    for pairs, start, whole in groups:
        acc, own = forward(meta, pairs, start, qg, whole, bias)
        stats = [own] + [back(own, steps) for steps in (1, 2, 3)]
        dkv, dqa = backward(meta, pairs, start, qg, whole, bias, acc, stats)
        dkv = dkv.reshape(NS * 2 * BLK, pairs * BLK)
        if start == 0:
            dkv = lax.psum_scatter(dkv, plane, scatter_dimension=0, tiled=True)
        else:
            dkv = lax.all_to_all(dkv, plane, 0, 0, tiled=True)
            dkv = jnp.sum(dkv.reshape(CHIPS, 4 * BLK, -1).astype(f32), axis=0).astype(bf16)
        sources.append(dkv.reshape(2, 2, BLK, -1))
        targets.append(z_sum(dqa))
    attended, grad_query = own_blocks(jnp.concatenate(targets, axis=-1), side)
    sources = jnp.concatenate(sources, axis=-1).transpose(1, 0, 2, 3)
    grad_key, grad_value = own_blocks(sources, side)
    return (attended, grad_query, grad_key, grad_value)


def solution(mesh):
    fine = Mesh(mesh.devices.reshape(4, 4, 2, 4), ("y", "x", "k", "z"))
    row = ("y", "x", "k")
    target = P(row + ("z",), None)
    source = P(("z",) + row, None)
    tile = P(row, "z")
    return jax.shard_map(
        shards,
        mesh=fine,
        in_specs=(target, source, source, target, tile, tile),
        out_specs=(target, target, source, source),
        check_vma=False,
    )
```

```python
import functools
import math

import jax
import jax.numpy as jnp
from jax import lax
from jax.experimental import pallas as pl
from jax.experimental.pallas import tpu as pltpu
from jax.sharding import Mesh
from jax.sharding import PartitionSpec as P

D = 1024
HEADS = 16
BLK = 128
HEAD = D // HEADS
HALF = D // 2
NT = 8
NS = 32
CHIPS = NS // 2
MAXT = 32
GROUPS = (3, 1)
LOW = -1e30
BASE2 = math.log2(math.e) / math.sqrt(HEAD)
SCALE = 1.0 / math.sqrt(HEAD)
f32 = jnp.float32
bf16 = jnp.bfloat16
VMEM = 56 * 1024 * 1024
EMPTY = 2 * MAXT


def dot(a, b):
    return jnp.dot(a, b, preferred_element_type=f32)


def cols(pp):
    return slice(pp * BLK, (pp + 1) * BLK)


def wide(first, second):
    return jnp.concatenate([first, second], axis=1)


def tall(first, second):
    return jnp.concatenate([first, second], axis=0)


def split_rows(tile):
    lane = lax.broadcasted_iota(jnp.int32, tile.shape, 1)
    zero = jnp.zeros_like(tile)
    return tall(jnp.where(lane < HEAD, tile, zero), jnp.where(lane >= HEAD, tile, zero))


def split_cols(tile):
    turned = tile.T
    zero = jnp.zeros((HEAD, BLK), tile.dtype)
    return wide(tall(turned[:HEAD], zero), tall(zero, turned[HEAD:]))


def bias_kernel(adj, mask_ref, out_ref, slot):
    row = pl.program_id(0)

    @pl.when(row == 0)
    def _():
        slot[0] = 0
        out_ref[...] = jnp.full(out_ref.shape, LOW, bf16)

    for s in range(NS):

        @pl.when(adj[row, s] > 0)
        def _():
            edge = mask_ref[:, s * BLK : (s + 1) * BLK]
            tile = jnp.where(edge > 0, 0.0, LOW).astype(f32)
            out_ref[jnp.minimum(slot[0], MAXT - 1)] = tile.T.astype(bf16)
            slot[0] = slot[0] + 1


def bias_tiles(adjacency, edge_mask):
    return pl.pallas_call(
        bias_kernel,
        grid_spec=pltpu.PrefetchScalarGridSpec(
            num_scalar_prefetch=1,
            grid=(4,),
            in_specs=[pl.BlockSpec((BLK, NS * BLK), lambda i, s: (i, 0))],
            out_specs=pl.BlockSpec((MAXT, BLK, BLK), lambda i, s: (0, 0, 0)),
            scratch_shapes=[pltpu.SMEM((1,), jnp.int32)],
        ),
        out_shape=jax.ShapeDtypeStruct((MAXT, BLK, BLK), bf16),
        compiler_params=pltpu.CompilerParams(vmem_limit_bytes=VMEM),
        cost_estimate=pl.CostEstimate(flops=0, bytes_accessed=30 * 2**20, transcendentals=0),
        name="bias_tiles",
    )(adjacency, edge_mask)


def block(meta, lt, slot):
    index = meta[2 * NT + lt * NS + slot]
    return index // 2, index % 2


def tiles(meta, lt, i):
    first = meta[NT + lt] + 2 * i
    second = jnp.where(2 * i + 1 < meta[lt], first + 1, EMPTY)
    return (block(meta, lt, 2 * i), block(meta, lt, 2 * i + 1)), (first, second)


def both_bias(bias_ref, places):
    bias = tall(bias_ref[places[0]], bias_ref[places[1]]).astype(f32)
    return wide(bias, bias)


def run(turns, step, state):
    state = lax.fori_loop(0, turns // 2, lambda j, held: step(2 * j + 1, step(2 * j, held)), state)
    return lax.fori_loop(0, turns % 2, lambda _, held: step(turns - 1, held), state)


def turn_blocks(pairs, turned_ref, ref):
    def turn(i, _):
        for j in range(4):
            for member in range(2):
                for pp in range(pairs):
                    chip = 4 * i + j
                    turned_ref[chip, member, cols(pp), :] = ref[chip, member, :, cols(pp)].T
        return 0

    lax.fori_loop(0, CHIPS // 4, turn, 0)


def rows_of(ref, blocks, pp):
    (c0, m0), (c1, m1) = blocks
    return tall(ref[c0, m0, :, cols(pp)], ref[c1, m1, :, cols(pp)])


def turned_of(ref, blocks, pp):
    (c0, m0), (c1, m1) = blocks
    return wide(ref[c0, m0, cols(pp), :], ref[c1, m1, cols(pp), :])


def add_rows(ref, blocks, kind, pp, part):
    for (chip, member), rows in zip(blocks, (part[:BLK], part[BLK:])):
        ref[kind, chip, member, :, cols(pp)] += rows


def forward_kernel(
    pairs, meta, qg_ref, key_ref, value_ref, bias_ref, acc_ref, stat_ref, vt_ref, query_ref, score_ref
):
    turn_blocks(pairs, vt_ref, value_ref)
    for lt in range(NT):
        for pp in range(pairs):
            query_ref[lt, pp] = split_cols(qg_ref[lt, 0, :, cols(pp)])

    def target(lt, _):
        turns = (meta[lt] + 1) // 2

        def score_step(i, tops):
            blocks, places = tiles(meta, lt, i)
            bias = both_bias(bias_ref, places)
            out = []
            for pp in range(pairs):
                keys = rows_of(key_ref, blocks, pp)
                scores = dot(keys, query_ref[lt, pp]) * BASE2 + bias
                score_ref[i, pp] = scores
                top = jnp.max(scores.reshape(-1, 8, 2 * BLK), axis=0)
                out.append(jnp.maximum(tops[pp], top))
            return tuple(out)

        tops = run(turns, score_step, tuple(jnp.full((8, 2 * BLK), LOW, f32) for _ in range(pairs)))
        tops = [jnp.max(top, axis=0, keepdims=True) for top in tops]

        def weight_step(i, state):
            blocks, _ = tiles(meta, lt, i)
            out = []
            for pp in range(pairs):
                total, acc = state[pp]
                weights = jnp.exp2(score_ref[i, pp] - tops[pp])
                total = total + jnp.sum(weights.reshape(-1, 8, 2 * BLK), axis=0)
                low = weights.astype(bf16)
                vt = turned_of(vt_ref, blocks, pp)
                part = wide(dot(vt[:HEAD], low[:, :BLK]), dot(vt[HEAD:], low[:, BLK:]))
                out.append((total, acc + part))
            return tuple(out)

        start = tuple(
            (jnp.zeros((8, 2 * BLK), f32), jnp.zeros((HEAD, 2 * BLK), f32)) for _ in range(pairs)
        )
        state = run(turns, weight_step, start)
        for pp in range(pairs):
            total, acc = state[pp]
            acc_ref[lt, pp] = acc
            stat_ref[pp, pl.ds(lt, 1), :] = tops[pp]
            stat_ref[pp, pl.ds(NT + lt, 1), :] = jnp.sum(total, axis=0, keepdims=True)
        return 0

    lax.fori_loop(0, NT, target, 0)
    for pp in range(pairs):
        deltas = []
        for lt in range(NT):
            grad = qg_ref[lt, 1, :, cols(pp)].T.astype(f32)
            grad = wide(grad[:HEAD], grad[HEAD:])
            deltas.append(jnp.sum(acc_ref[lt, pp] * grad, axis=0, keepdims=True))
        stat_ref[pp, 2 * NT :, :] = jnp.concatenate(deltas)


def spec(shape, *index):
    return pl.BlockSpec(shape, lambda p, s: index, pipeline_mode=pl.Buffered(1))


def specs(pairs, start):
    width = pairs * BLK
    return (
        spec((NT, 2, BLK, width), 0, 0, 0, start // pairs),
        [spec((CHIPS, None, 2, BLK, width), 0, kind, 0, 0, 0) for kind in range(2)],
        spec((EMPTY + 1, BLK, BLK), 0, 0, 0),
        spec((NT, pairs, HEAD, 2 * BLK), 0, 0, 0, 0),
        spec((pairs, 3 * NT, 2 * BLK), 0, 0, 0),
    )


def forward(meta, pairs, start, qg, kv, bias):
    qg_spec, kv_specs, bias_spec, acc_spec, stat_spec = specs(pairs, start)
    return pl.pallas_call(
        functools.partial(forward_kernel, pairs),
        grid_spec=pltpu.PrefetchScalarGridSpec(
            num_scalar_prefetch=1,
            grid=(1,),
            in_specs=[qg_spec] + kv_specs + [bias_spec],
            out_specs=[acc_spec, stat_spec],
            scratch_shapes=[
                pltpu.VMEM((CHIPS, 2, pairs * BLK, BLK), bf16),
                pltpu.VMEM((NT, pairs, BLK, 2 * BLK), bf16),
                pltpu.VMEM((NS // 2, pairs, 2 * BLK, 2 * BLK), f32),
            ],
        ),
        out_shape=[
            jax.ShapeDtypeStruct((NT, pairs, HEAD, 2 * BLK), f32),
            jax.ShapeDtypeStruct((pairs, 3 * NT, 2 * BLK), f32),
        ],
        compiler_params=pltpu.CompilerParams(vmem_limit_bytes=VMEM),
        cost_estimate=pl.CostEstimate(
            flops=10**10, bytes_accessed=20 * 2**20, transcendentals=10**7
        ),
        name="forward" + str(start),
    )(meta, qg, kv, kv, bias)


def backward_kernel(
    pairs, meta, qg_ref, key_ref, value_ref, bias_ref, acc_ref, own_ref, one_ref, two_ref, three_ref,
    dkv_ref, dqa_ref, kt_ref, turned_ref, dq_ref, sum_ref, row_ref,
):
    turn_blocks(pairs, kt_ref, key_ref)
    for lt in range(NT):
        for pp in range(pairs):
            for kind in range(2):
                turned_ref[lt, pp, kind] = split_cols(qg_ref[lt, kind, :, cols(pp)])
    sum_ref[...] = jnp.zeros_like(sum_ref)
    for pp in range(pairs):
        parts = []
        for back, ref in enumerate((own_ref, one_ref, two_ref, three_ref)):
            stat = [ref[pp, part * NT : (part + 1) * NT, :] for part in range(3)]
            if back:
                stat = [pltpu.roll(rows, 2 * back, 0) for rows in stat]
            parts.append(stat)
        top = jnp.maximum(
            jnp.maximum(parts[0][0], parts[1][0]), jnp.maximum(parts[2][0], parts[3][0])
        )
        factors = [jnp.exp2(stat[0] - top) for stat in parts]
        total = sum(stat[1] * factor for stat, factor in zip(parts, factors))
        delta = sum(stat[2] * factor for stat, factor in zip(parts, factors))
        log_total = top + jnp.log2(total)
        row_ref[pp, :NT, :] = log_total
        row_ref[pp, NT : 2 * NT, :] = delta / total
        row_ref[pp, 2 * NT :, :] = jnp.exp2(parts[0][0] - log_total)

    def target(lt, _):
        rows = [
            [split_rows(qg_ref[lt, kind, :, cols(pp)]) for kind in range(2)] for pp in range(pairs)
        ]
        log_totals = [row_ref[pp, pl.ds(lt, 1), :] for pp in range(pairs)]
        deltas = [row_ref[pp, pl.ds(NT + lt, 1), :] for pp in range(pairs)]

        def step(i, state):
            blocks, places = tiles(meta, lt, i)
            bias = both_bias(bias_ref, places)
            out = []
            for pp in range(pairs):
                keys = rows_of(key_ref, blocks, pp)
                values = rows_of(value_ref, blocks, pp)
                scores = dot(keys, turned_ref[lt, pp, 0]) * BASE2 + bias
                probs = jnp.exp2(scores - log_totals[pp])
                grad_prob = dot(values, turned_ref[lt, pp, 1])
                grad_score = (probs * (grad_prob - deltas[pp])).astype(bf16)
                value_part = dot(probs.astype(bf16), rows[pp][1])
                key_part = dot(grad_score, rows[pp][0])
                add_rows(sum_ref, blocks, 0, pp, key_part)
                add_rows(sum_ref, blocks, 1, pp, value_part)
                kt = turned_of(kt_ref, blocks, pp)
                part = wide(
                    dot(kt[:HEAD], grad_score[:, :BLK]), dot(kt[HEAD:], grad_score[:, BLK:])
                )
                out.append(state[pp] + part)
            return tuple(out)

        start = tuple(jnp.zeros((HEAD, 2 * BLK), f32) for _ in range(pairs))
        state = run((meta[lt] + 1) // 2, step, start)
        for pp in range(pairs):
            dq_ref[lt, pp] = state[pp] * SCALE
        return 0

    lax.fori_loop(0, NT, target, 0)

    def finish(i, _):
        for lt in (2 * i, 2 * i + 1):
            for pp in range(pairs):
                attended = acc_ref[lt, pp] * row_ref[pp, pl.ds(2 * NT + lt, 1), :]
                for kind, pair in enumerate((attended, dq_ref[lt, pp])):
                    pair = tall(pair[:, :BLK], pair[:, BLK:])
                    dqa_ref[lt, kind, :, cols(pp)] = pair.T.astype(bf16)
        return 0

    lax.fori_loop(0, NT // 2, finish, 0)
    dkv_ref[:, 0] = (sum_ref[0] * SCALE).astype(bf16)
    dkv_ref[:, 1] = sum_ref[1].astype(bf16)


def backward(meta, pairs, start, qg, kv, bias, acc, stats):
    qg_spec, kv_specs, bias_spec, acc_spec, stat_spec = specs(pairs, start)
    width = pairs * BLK
    return pl.pallas_call(
        functools.partial(backward_kernel, pairs),
        grid_spec=pltpu.PrefetchScalarGridSpec(
            num_scalar_prefetch=1,
            grid=(1,),
            in_specs=[qg_spec] + kv_specs + [bias_spec, acc_spec] + [stat_spec] * 4,
            out_specs=[
                spec((CHIPS, 2, 2, BLK, width), 0, 0, 0, 0, 0),
                spec((NT, 2, BLK, width), 0, 0, 0, 0),
            ],
            scratch_shapes=[
                pltpu.VMEM((CHIPS, 2, width, BLK), bf16),
                pltpu.VMEM((NT, pairs, 2, BLK, 2 * BLK), bf16),
                pltpu.VMEM((NT, pairs, HEAD, 2 * BLK), f32),
                pltpu.VMEM((2, CHIPS, 2, BLK, width), f32),
                pltpu.VMEM((pairs, 3 * NT, 2 * BLK), f32),
            ],
        ),
        out_shape=[
            jax.ShapeDtypeStruct((CHIPS, 2, 2, BLK, width), bf16),
            jax.ShapeDtypeStruct((NT, 2, BLK, width), bf16),
        ],
        compiler_params=pltpu.CompilerParams(vmem_limit_bytes=VMEM),
        cost_estimate=pl.CostEstimate(
            flops=2 * 10**10, bytes_accessed=30 * 2**20, transcendentals=10**7
        ),
        name="backward" + str(start),
    )(meta, qg, kv, kv, bias, acc, *stats)


def steps_back(rows, z):
    turned = jnp.concatenate([rows[:1], rows[3:], rows[2:3], rows[1:2]])
    return lax.dynamic_slice_in_dim(jnp.concatenate([turned, turned]), 4 - z, 4)


def tile_lists(own_adj, got_adj, side, z):
    adj = jnp.stack([own_adj, got_adj], axis=1)
    count = jnp.sum(adj, axis=2)
    first = jnp.cumsum(count, axis=0) - count + jnp.array([0, MAXT])
    adj = steps_back(adj, z).reshape(NT, NS)
    count = steps_back(count, z).reshape(NT)
    first = steps_back(first, z).reshape(NT)
    place = jnp.cumsum(adj, axis=1) - 1
    hit = (adj[:, None, :] > 0) & (place[:, None, :] == jnp.arange(NS)[None, :, None])
    held = jnp.arange(NS) ^ side
    source = jnp.sum(jnp.where(hit, held[None, None, :], 0), axis=2)
    return jnp.concatenate([count, first, source.reshape(-1)]).astype(jnp.int32)


SWAP = [(0, 1), (1, 0)]


def back(array, steps, axis="z"):
    return lax.ppermute(array, axis, [(s, (s + steps) % 4) for s in range(4)])


def half(array, side):
    return lax.dynamic_slice_in_dim(array, side * HALF, HALF, array.ndim - 1)


def chip_pair(first, second, side, axis):
    both = jnp.stack([first, second])
    got = lax.ppermute(half(both, 1 - side), "k", SWAP)
    return jnp.stack([half(both, side), got], axis=axis)


def ring_reduce(parts, axis):
    here = lax.axis_index(axis)
    own, right, far, left = (
        lax.dynamic_index_in_dim(parts, (here + steps) % 4, 0, False) for steps in range(4)
    )
    middle = far.shape[0] // 2
    onward = back(far[:middle], 1, axis)
    backward_half = back(far[middle:], -1, axis)

    def add(mine, got):
        return (mine.astype(f32) + got.astype(f32)).astype(bf16)

    right = jnp.concatenate([add(right[:middle], onward), right[middle:]])
    left = jnp.concatenate([left[:middle], add(left[middle:], backward_half)])
    right, left = back(right, 1, axis), back(left, -1, axis)
    return own.astype(f32) + right.astype(f32) + left.astype(f32)


def plane_sum(parts):
    rows = ring_reduce(parts.reshape(4, 4 * 4 * BLK, -1), "y").astype(bf16)
    return ring_reduce(rows.reshape(4, 4 * BLK, -1), "x").astype(bf16)


def own_blocks(part, side):
    got = lax.ppermute(part[1], "k", SWAP)
    whole = jnp.where(
        side == 0,
        jnp.concatenate([part[0], got], axis=-1),
        jnp.concatenate([got, part[0]], axis=-1),
    )
    return whole[0], whole[1]


def z_sum(part):
    part = part.reshape(4, 2, 2, BLK, -1)
    total = part[0].astype(f32)
    for steps in (1, 2, 3):
        total = total + back(part[steps], -steps).astype(f32)
    return total.astype(bf16)


def shards(node_query, node_key, node_value, grad_out, block_adjacency, edge_mask):
    side, z = lax.axis_index("k"), lax.axis_index("z")
    plane = ("y", "x")
    kv = chip_pair(node_key, node_value, side, 1)
    groups, start = [], 0
    for pairs in GROUPS:
        width = pairs * BLK
        part = kv[..., start * BLK : start * BLK + width].reshape(4 * BLK, width)
        whole = lax.all_gather(part, plane, axis=0, tiled=True)
        groups.append((pairs, start, whole.reshape(CHIPS, 2, 2, BLK, width)))
        start += pairs
    qg = chip_pair(node_query, grad_out, side, 0).reshape(4 * BLK, HALF)
    qg = jnp.concatenate([qg] + [back(qg, steps) for steps in (1, 2, 3)])
    qg = qg.reshape(NT, 2, BLK, HALF)
    own_adj = (block_adjacency > 0).astype(jnp.int32)
    own_bias = bias_tiles(own_adj, edge_mask)
    got_bias = lax.ppermute(own_bias, "k", SWAP)
    bias = jnp.concatenate([own_bias, got_bias, jnp.full((1, BLK, BLK), LOW, bf16)])
    got_adj = lax.ppermute(own_adj, "k", SWAP)
    meta = tile_lists(own_adj, got_adj, side, z)
    sources, targets = [], []
    for pairs, start, whole in groups:
        acc, own = forward(meta, pairs, start, qg, whole, bias)
        stats = [own] + [back(own, steps) for steps in (1, 2, 3)]
        dkv, dqa = backward(meta, pairs, start, qg, whole, bias, acc, stats)
        dkv = dkv.reshape(NS * 2 * BLK, pairs * BLK)
        if start == 0:
            dkv = lax.psum_scatter(dkv, plane, scatter_dimension=0, tiled=True)
        else:
            dkv = plane_sum(dkv)
        sources.append(dkv.reshape(2, 2, BLK, -1))
        targets.append(z_sum(dqa))
    attended, grad_query = own_blocks(jnp.concatenate(targets, axis=-1), side)
    sources = jnp.concatenate(sources, axis=-1).transpose(1, 0, 2, 3)
    grad_key, grad_value = own_blocks(sources, side)
    return (attended, grad_query, grad_key, grad_value)


def solution(mesh):
    fine = Mesh(mesh.devices.reshape(4, 4, 2, 4), ("y", "x", "k", "z"))
    row = ("y", "x", "k")
    target = P(row + ("z",), None)
    source = P(("z",) + row, None)
    tile = P(row, "z")
    return jax.shard_map(
        shards,
        mesh=fine,
        in_specs=(target, source, source, target, tile, tile),
        out_specs=(target, target, source, source),
        check_vma=False,
    )
```

```python
import functools
import math

import jax
import jax.numpy as jnp
from jax import lax
from jax.experimental import pallas as pl
from jax.experimental.pallas import tpu as pltpu
from jax.sharding import Mesh
from jax.sharding import PartitionSpec as P

D = 1024
HEADS = 16
BLK = 128
HEAD = D // HEADS
HALF = D // 2
NT = 8
NS = 32
CHIPS = NS // 2
MAXT = 32
GROUPS = (3, 1)
LOW = -1e30
BASE2 = math.log2(math.e) / math.sqrt(HEAD)
SCALE = 1.0 / math.sqrt(HEAD)
f32 = jnp.float32
bf16 = jnp.bfloat16
VMEM = 56 * 1024 * 1024
EMPTY = 2 * MAXT


def dot(a, b):
    return jnp.dot(a, b, preferred_element_type=f32)


def cols(pp):
    return slice(pp * BLK, (pp + 1) * BLK)


def wide(first, second):
    return jnp.concatenate([first, second], axis=1)


def tall(first, second):
    return jnp.concatenate([first, second], axis=0)


def split_rows(tile):
    lane = lax.broadcasted_iota(jnp.int32, tile.shape, 1)
    zero = jnp.zeros_like(tile)
    return tall(jnp.where(lane < HEAD, tile, zero), jnp.where(lane >= HEAD, tile, zero))


def split_cols(tile):
    turned = tile.T
    zero = jnp.zeros((HEAD, BLK), tile.dtype)
    return wide(tall(turned[:HEAD], zero), tall(zero, turned[HEAD:]))


def bias_kernel(adj, mask_ref, out_ref, slot):
    row = pl.program_id(0)

    @pl.when(row == 0)
    def _():
        slot[0] = 0
        out_ref[...] = jnp.full(out_ref.shape, LOW, bf16)

    for s in range(NS):

        @pl.when(adj[row, s] > 0)
        def _():
            edge = mask_ref[:, s * BLK : (s + 1) * BLK]
            tile = jnp.where(edge > 0, 0.0, LOW).astype(f32)
            out_ref[jnp.minimum(slot[0], MAXT - 1)] = tile.T.astype(bf16)
            slot[0] = slot[0] + 1


def bias_tiles(adjacency, edge_mask):
    return pl.pallas_call(
        bias_kernel,
        grid_spec=pltpu.PrefetchScalarGridSpec(
            num_scalar_prefetch=1,
            grid=(4,),
            in_specs=[pl.BlockSpec((BLK, NS * BLK), lambda i, s: (i, 0))],
            out_specs=pl.BlockSpec((MAXT, BLK, BLK), lambda i, s: (0, 0, 0)),
            scratch_shapes=[pltpu.SMEM((1,), jnp.int32)],
        ),
        out_shape=jax.ShapeDtypeStruct((MAXT, BLK, BLK), bf16),
        compiler_params=pltpu.CompilerParams(vmem_limit_bytes=VMEM),
        cost_estimate=pl.CostEstimate(flops=0, bytes_accessed=30 * 2**20, transcendentals=0),
        name="bias_tiles",
    )(adjacency, edge_mask)


def block(meta, lt, slot):
    index = meta[2 * NT + lt * NS + slot]
    return index // 2, index % 2


def tiles(meta, lt, i):
    first = meta[NT + lt] + 2 * i
    second = jnp.where(2 * i + 1 < meta[lt], first + 1, EMPTY)
    return (block(meta, lt, 2 * i), block(meta, lt, 2 * i + 1)), (first, second)


def both_bias(bias_ref, places):
    bias = tall(bias_ref[places[0]], bias_ref[places[1]]).astype(f32)
    return wide(bias, bias)


def run(turns, step, state):
    state = lax.fori_loop(0, turns // 2, lambda j, held: step(2 * j + 1, step(2 * j, held)), state)
    return lax.fori_loop(0, turns % 2, lambda _, held: step(turns - 1, held), state)


def turn_blocks(pairs, turned_ref, ref):
    def turn(i, _):
        for j in range(4):
            for member in range(2):
                for pp in range(pairs):
                    chip = 4 * i + j
                    turned_ref[chip, member, cols(pp), :] = ref[chip, member, :, cols(pp)].T
        return 0

    lax.fori_loop(0, CHIPS // 4, turn, 0)


def rows_of(ref, blocks, pp):
    (c0, m0), (c1, m1) = blocks
    return tall(ref[c0, m0, :, cols(pp)], ref[c1, m1, :, cols(pp)])


def turned_of(ref, blocks, pp):
    (c0, m0), (c1, m1) = blocks
    return wide(ref[c0, m0, cols(pp), :], ref[c1, m1, cols(pp), :])


def add_rows(ref, blocks, kind, pp, part):
    for (chip, member), rows in zip(blocks, (part[:BLK], part[BLK:])):
        ref[kind, chip, member, :, cols(pp)] += rows


def forward_kernel(
    pairs, meta, qg_ref, key_ref, value_ref, bias_ref, acc_ref, stat_ref, vt_ref, query_ref, score_ref
):
    turn_blocks(pairs, vt_ref, value_ref)
    for lt in range(NT):
        for pp in range(pairs):
            query_ref[lt, pp] = split_cols(qg_ref[lt, 0, :, cols(pp)])

    def target(lt, _):
        turns = (meta[lt] + 1) // 2

        def score_step(i, tops):
            blocks, places = tiles(meta, lt, i)
            bias = both_bias(bias_ref, places)
            out = []
            for pp in range(pairs):
                keys = rows_of(key_ref, blocks, pp)
                scores = dot(keys, query_ref[lt, pp]) * BASE2 + bias
                score_ref[i, pp] = scores
                top = jnp.max(scores.reshape(-1, 8, 2 * BLK), axis=0)
                out.append(jnp.maximum(tops[pp], top))
            return tuple(out)

        tops = run(turns, score_step, tuple(jnp.full((8, 2 * BLK), LOW, f32) for _ in range(pairs)))
        tops = [jnp.max(top, axis=0, keepdims=True) for top in tops]

        def weight_step(i, state):
            blocks, _ = tiles(meta, lt, i)
            out = []
            for pp in range(pairs):
                total, acc = state[pp]
                weights = jnp.exp2(score_ref[i, pp] - tops[pp])
                total = total + jnp.sum(weights.reshape(-1, 8, 2 * BLK), axis=0)
                low = weights.astype(bf16)
                vt = turned_of(vt_ref, blocks, pp)
                part = wide(dot(vt[:HEAD], low[:, :BLK]), dot(vt[HEAD:], low[:, BLK:]))
                out.append((total, acc + part))
            return tuple(out)

        start = tuple(
            (jnp.zeros((8, 2 * BLK), f32), jnp.zeros((HEAD, 2 * BLK), f32)) for _ in range(pairs)
        )
        state = run(turns, weight_step, start)
        for pp in range(pairs):
            total, acc = state[pp]
            acc_ref[lt, pp] = acc
            stat_ref[pp, pl.ds(lt, 1), :] = tops[pp]
            stat_ref[pp, pl.ds(NT + lt, 1), :] = jnp.sum(total, axis=0, keepdims=True)
        return 0

    lax.fori_loop(0, NT, target, 0)
    for pp in range(pairs):
        deltas = []
        for lt in range(NT):
            grad = qg_ref[lt, 1, :, cols(pp)].T.astype(f32)
            grad = wide(grad[:HEAD], grad[HEAD:])
            deltas.append(jnp.sum(acc_ref[lt, pp] * grad, axis=0, keepdims=True))
        stat_ref[pp, 2 * NT :, :] = jnp.concatenate(deltas)


def spec(shape, *index):
    return pl.BlockSpec(shape, lambda p, s: index, pipeline_mode=pl.Buffered(1))


def specs(pairs, start):
    width = pairs * BLK
    return (
        spec((NT, 2, BLK, width), 0, 0, 0, start // pairs),
        [spec((CHIPS, None, 2, BLK, width), 0, kind, 0, 0, 0) for kind in range(2)],
        spec((EMPTY + 1, BLK, BLK), 0, 0, 0),
        spec((NT, pairs, HEAD, 2 * BLK), 0, 0, 0, 0),
        spec((pairs, 3 * NT, 2 * BLK), 0, 0, 0),
    )


def forward(meta, pairs, start, qg, kv, bias):
    qg_spec, kv_specs, bias_spec, acc_spec, stat_spec = specs(pairs, start)
    return pl.pallas_call(
        functools.partial(forward_kernel, pairs),
        grid_spec=pltpu.PrefetchScalarGridSpec(
            num_scalar_prefetch=1,
            grid=(1,),
            in_specs=[qg_spec] + kv_specs + [bias_spec],
            out_specs=[acc_spec, stat_spec],
            scratch_shapes=[
                pltpu.VMEM((CHIPS, 2, pairs * BLK, BLK), bf16),
                pltpu.VMEM((NT, pairs, BLK, 2 * BLK), bf16),
                pltpu.VMEM((NS // 2, pairs, 2 * BLK, 2 * BLK), f32),
            ],
        ),
        out_shape=[
            jax.ShapeDtypeStruct((NT, pairs, HEAD, 2 * BLK), f32),
            jax.ShapeDtypeStruct((pairs, 3 * NT, 2 * BLK), f32),
        ],
        compiler_params=pltpu.CompilerParams(vmem_limit_bytes=VMEM),
        cost_estimate=pl.CostEstimate(
            flops=10**10, bytes_accessed=20 * 2**20, transcendentals=10**7
        ),
        name="forward" + str(start),
    )(meta, qg, kv, kv, bias)


def backward_kernel(
    pairs, meta, qg_ref, key_ref, value_ref, bias_ref, acc_ref, own_ref, one_ref, two_ref, three_ref,
    dkv_ref, dqa_ref, kt_ref, turned_ref, dq_ref, sum_ref, row_ref,
):
    turn_blocks(pairs, kt_ref, key_ref)
    for lt in range(NT):
        for pp in range(pairs):
            for kind in range(2):
                turned_ref[lt, pp, kind] = split_cols(qg_ref[lt, kind, :, cols(pp)])
    sum_ref[...] = jnp.zeros_like(sum_ref)
    for pp in range(pairs):
        parts = []
        for back, ref in enumerate((own_ref, one_ref, two_ref, three_ref)):
            stat = [ref[pp, part * NT : (part + 1) * NT, :] for part in range(3)]
            if back:
                stat = [pltpu.roll(rows, 2 * back, 0) for rows in stat]
            parts.append(stat)
        top = jnp.maximum(
            jnp.maximum(parts[0][0], parts[1][0]), jnp.maximum(parts[2][0], parts[3][0])
        )
        factors = [jnp.exp2(stat[0] - top) for stat in parts]
        total = sum(stat[1] * factor for stat, factor in zip(parts, factors))
        delta = sum(stat[2] * factor for stat, factor in zip(parts, factors))
        log_total = top + jnp.log2(total)
        row_ref[pp, :NT, :] = log_total
        row_ref[pp, NT : 2 * NT, :] = delta / total
        row_ref[pp, 2 * NT :, :] = jnp.exp2(parts[0][0] - log_total)

    def target(lt, _):
        rows = [
            [split_rows(qg_ref[lt, kind, :, cols(pp)]) for kind in range(2)] for pp in range(pairs)
        ]
        log_totals = [row_ref[pp, pl.ds(lt, 1), :] for pp in range(pairs)]
        deltas = [row_ref[pp, pl.ds(NT + lt, 1), :] for pp in range(pairs)]

        def step(i, state):
            blocks, places = tiles(meta, lt, i)
            bias = both_bias(bias_ref, places)
            out = []
            for pp in range(pairs):
                keys = rows_of(key_ref, blocks, pp)
                values = rows_of(value_ref, blocks, pp)
                scores = dot(keys, turned_ref[lt, pp, 0]) * BASE2 + bias
                probs = jnp.exp2(scores - log_totals[pp])
                grad_prob = dot(values, turned_ref[lt, pp, 1])
                grad_score = (probs * (grad_prob - deltas[pp])).astype(bf16)
                value_part = dot(probs.astype(bf16), rows[pp][1])
                key_part = dot(grad_score, rows[pp][0])
                add_rows(sum_ref, blocks, 0, pp, key_part)
                add_rows(sum_ref, blocks, 1, pp, value_part)
                kt = turned_of(kt_ref, blocks, pp)
                part = wide(
                    dot(kt[:HEAD], grad_score[:, :BLK]), dot(kt[HEAD:], grad_score[:, BLK:])
                )
                out.append(state[pp] + part)
            return tuple(out)

        start = tuple(jnp.zeros((HEAD, 2 * BLK), f32) for _ in range(pairs))
        state = run((meta[lt] + 1) // 2, step, start)
        for pp in range(pairs):
            dq_ref[lt, pp] = state[pp] * SCALE
        return 0

    lax.fori_loop(0, NT, target, 0)

    def finish(i, _):
        for lt in (2 * i, 2 * i + 1):
            for pp in range(pairs):
                attended = acc_ref[lt, pp] * row_ref[pp, pl.ds(2 * NT + lt, 1), :]
                for kind, pair in enumerate((attended, dq_ref[lt, pp])):
                    pair = tall(pair[:, :BLK], pair[:, BLK:])
                    dqa_ref[lt, kind, :, cols(pp)] = pair.T.astype(bf16)
        return 0

    lax.fori_loop(0, NT // 2, finish, 0)
    dkv_ref[:, 0] = (sum_ref[0] * SCALE).astype(bf16)
    dkv_ref[:, 1] = sum_ref[1].astype(bf16)


def backward(meta, pairs, start, qg, kv, bias, acc, stats):
    qg_spec, kv_specs, bias_spec, acc_spec, stat_spec = specs(pairs, start)
    width = pairs * BLK
    return pl.pallas_call(
        functools.partial(backward_kernel, pairs),
        grid_spec=pltpu.PrefetchScalarGridSpec(
            num_scalar_prefetch=1,
            grid=(1,),
            in_specs=[qg_spec] + kv_specs + [bias_spec, acc_spec] + [stat_spec] * 4,
            out_specs=[
                spec((CHIPS, 2, 2, BLK, width), 0, 0, 0, 0, 0),
                spec((NT, 2, BLK, width), 0, 0, 0, 0),
            ],
            scratch_shapes=[
                pltpu.VMEM((CHIPS, 2, width, BLK), bf16),
                pltpu.VMEM((NT, pairs, 2, BLK, 2 * BLK), bf16),
                pltpu.VMEM((NT, pairs, HEAD, 2 * BLK), f32),
                pltpu.VMEM((2, CHIPS, 2, BLK, width), f32),
                pltpu.VMEM((pairs, 3 * NT, 2 * BLK), f32),
            ],
        ),
        out_shape=[
            jax.ShapeDtypeStruct((CHIPS, 2, 2, BLK, width), bf16),
            jax.ShapeDtypeStruct((NT, 2, BLK, width), bf16),
        ],
        compiler_params=pltpu.CompilerParams(vmem_limit_bytes=VMEM),
        cost_estimate=pl.CostEstimate(
            flops=2 * 10**10, bytes_accessed=30 * 2**20, transcendentals=10**7
        ),
        name="backward" + str(start),
    )(meta, qg, kv, kv, bias, acc, *stats)


def steps_back(rows, z):
    turned = jnp.concatenate([rows[:1], rows[3:], rows[2:3], rows[1:2]])
    return lax.dynamic_slice_in_dim(jnp.concatenate([turned, turned]), 4 - z, 4)


def tile_lists(own_adj, got_adj, side, z):
    adj = jnp.stack([own_adj, got_adj], axis=1)
    count = jnp.sum(adj, axis=2)
    first = jnp.cumsum(count, axis=0) - count + jnp.array([0, MAXT])
    adj = steps_back(adj, z).reshape(NT, NS)
    count = steps_back(count, z).reshape(NT)
    first = steps_back(first, z).reshape(NT)
    place = jnp.cumsum(adj, axis=1) - 1
    hit = (adj[:, None, :] > 0) & (place[:, None, :] == jnp.arange(NS)[None, :, None])
    held = jnp.arange(NS) ^ side
    source = jnp.sum(jnp.where(hit, held[None, None, :], 0), axis=2)
    return jnp.concatenate([count, first, source.reshape(-1)]).astype(jnp.int32)


SWAP = [(0, 1), (1, 0)]


def back(array, steps, axis="z"):
    return lax.ppermute(array, axis, [(s, (s + steps) % 4) for s in range(4)])


def half(array, side):
    return lax.dynamic_slice_in_dim(array, side * HALF, HALF, array.ndim - 1)


def chip_pair(first, second, side, axis):
    both = jnp.stack([first, second])
    got = lax.ppermute(half(both, 1 - side), "k", SWAP)
    return jnp.stack([half(both, side), got], axis=axis)


def ring_reduce(parts, axis):
    here = lax.axis_index(axis)
    own, right, far, left = (
        lax.dynamic_index_in_dim(parts, (here + steps) % 4, 0, False) for steps in range(4)
    )
    middle = far.shape[0] // 2
    onward = back(far[:middle], 1, axis)
    backward_half = back(far[middle:], -1, axis)

    def add(mine, got):
        return (mine.astype(f32) + got.astype(f32)).astype(bf16)

    right = jnp.concatenate([add(right[:middle], onward), right[middle:]])
    left = jnp.concatenate([left[:middle], add(left[middle:], backward_half)])
    right, left = back(right, 1, axis), back(left, -1, axis)
    return own.astype(f32) + right.astype(f32) + left.astype(f32)


def plane_sum(parts):
    rows = ring_reduce(parts.reshape(4, 4 * 4 * BLK, -1), "y").astype(bf16)
    return ring_reduce(rows.reshape(4, 4 * BLK, -1), "x").astype(bf16)


def own_blocks(part, side):
    got = lax.ppermute(part[1], "k", SWAP)
    whole = jnp.where(
        side == 0,
        jnp.concatenate([part[0], got], axis=-1),
        jnp.concatenate([got, part[0]], axis=-1),
    )
    return whole[0], whole[1]


def z_sum(part):
    part = part.reshape(4, 2, 2, BLK, -1)
    total = part[0].astype(f32)
    for steps in (1, 2, 3):
        total = total + back(part[steps], -steps).astype(f32)
    return total.astype(bf16)


def shards(node_query, node_key, node_value, grad_out, block_adjacency, edge_mask):
    side, z = lax.axis_index("k"), lax.axis_index("z")
    plane = ("y", "x")
    kv = chip_pair(node_key, node_value, side, 1)
    groups, start = [], 0
    for pairs in GROUPS:
        width = pairs * BLK
        part = kv[..., start * BLK : start * BLK + width].reshape(4 * BLK, width)
        whole = lax.all_gather(part, plane, axis=0, tiled=True)
        groups.append((pairs, start, whole.reshape(CHIPS, 2, 2, BLK, width)))
        start += pairs
    qg = chip_pair(node_query, grad_out, side, 0).reshape(4 * BLK, HALF)
    qg = jnp.concatenate([qg] + [back(qg, steps) for steps in (1, 2, 3)])
    qg = qg.reshape(NT, 2, BLK, HALF)
    own_adj = (block_adjacency > 0).astype(jnp.int32)
    own_bias = bias_tiles(own_adj, edge_mask)
    got_bias = lax.ppermute(own_bias, "k", SWAP)
    bias = jnp.concatenate([own_bias, got_bias, jnp.full((1, BLK, BLK), LOW, bf16)])
    got_adj = lax.ppermute(own_adj, "k", SWAP)
    meta = tile_lists(own_adj, got_adj, side, z)
    sources, targets = [], []
    for pairs, start, whole in groups:
        acc, own = forward(meta, pairs, start, qg, whole, bias)
        stats = [own] + [back(own, steps) for steps in (1, 2, 3)]
        dkv, dqa = backward(meta, pairs, start, qg, whole, bias, acc, stats)
        dkv = dkv.reshape(NS * 2 * BLK, pairs * BLK)
        if start == 0:
            dkv = lax.psum_scatter(dkv, plane, scatter_dimension=0, tiled=True)
        else:
            dkv, targets[0] = lax.optimization_barrier((dkv, targets[0]))
            dkv = plane_sum(dkv)
        sources.append(dkv.reshape(2, 2, BLK, -1))
        targets.append(z_sum(dqa))
    attended, grad_query = own_blocks(jnp.concatenate(targets, axis=-1), side)
    sources = jnp.concatenate(sources, axis=-1).transpose(1, 0, 2, 3)
    grad_key, grad_value = own_blocks(sources, side)
    return (attended, grad_query, grad_key, grad_value)


def solution(mesh):
    fine = Mesh(mesh.devices.reshape(4, 4, 2, 4), ("y", "x", "k", "z"))
    row = ("y", "x", "k")
    target = P(row + ("z",), None)
    source = P(("z",) + row, None)
    tile = P(row, "z")
    return jax.shard_map(
        shards,
        mesh=fine,
        in_specs=(target, source, source, target, tile, tile),
        out_specs=(target, target, source, source),
        check_vma=False,
    )
```

```python
import functools
import math

import jax
import jax.numpy as jnp
from jax import lax
from jax.experimental import pallas as pl
from jax.experimental.pallas import tpu as pltpu
from jax.sharding import Mesh
from jax.sharding import PartitionSpec as P

D = 1024
HEADS = 16
BLK = 128
HEAD = D // HEADS
HALF = D // 2
NT = 8
NS = 32
CHIPS = NS // 2
MAXT = 32
GROUPS = (3, 1)
LOW = -1e30
BASE2 = math.log2(math.e) / math.sqrt(HEAD)
SCALE = 1.0 / math.sqrt(HEAD)
f32 = jnp.float32
bf16 = jnp.bfloat16
VMEM = 56 * 1024 * 1024
EMPTY = 2 * MAXT


def dot(a, b):
    return jnp.dot(a, b, preferred_element_type=f32)


def cols(pp):
    return slice(pp * BLK, (pp + 1) * BLK)


def wide(first, second):
    return jnp.concatenate([first, second], axis=1)


def tall(first, second):
    return jnp.concatenate([first, second], axis=0)


def split_rows(tile):
    lane = lax.broadcasted_iota(jnp.int32, tile.shape, 1)
    zero = jnp.zeros_like(tile)
    return tall(jnp.where(lane < HEAD, tile, zero), jnp.where(lane >= HEAD, tile, zero))


def split_cols(tile):
    turned = tile.T
    zero = jnp.zeros((HEAD, BLK), tile.dtype)
    return wide(tall(turned[:HEAD], zero), tall(zero, turned[HEAD:]))


def bias_kernel(adj, mask_ref, out_ref, slot):
    row = pl.program_id(0)

    @pl.when(row == 0)
    def _():
        slot[0] = 0
        out_ref[...] = jnp.full(out_ref.shape, LOW, bf16)

    for s in range(NS):

        @pl.when(adj[row, s] > 0)
        def _():
            edge = mask_ref[:, s * BLK : (s + 1) * BLK]
            tile = jnp.where(edge > 0, 0.0, LOW).astype(f32)
            out_ref[jnp.minimum(slot[0], MAXT - 1)] = tile.T.astype(bf16)
            slot[0] = slot[0] + 1


def bias_tiles(adjacency, edge_mask):
    return pl.pallas_call(
        bias_kernel,
        grid_spec=pltpu.PrefetchScalarGridSpec(
            num_scalar_prefetch=1,
            grid=(4,),
            in_specs=[pl.BlockSpec((BLK, NS * BLK), lambda i, s: (i, 0))],
            out_specs=pl.BlockSpec((MAXT, BLK, BLK), lambda i, s: (0, 0, 0)),
            scratch_shapes=[pltpu.SMEM((1,), jnp.int32)],
        ),
        out_shape=jax.ShapeDtypeStruct((MAXT, BLK, BLK), bf16),
        compiler_params=pltpu.CompilerParams(vmem_limit_bytes=VMEM),
        cost_estimate=pl.CostEstimate(flops=0, bytes_accessed=30 * 2**20, transcendentals=0),
        name="bias_tiles",
    )(adjacency, edge_mask)


def block(meta, lt, slot):
    index = meta[2 * NT + lt * NS + slot]
    return index // 2, index % 2


def tiles(meta, lt, i):
    first = meta[NT + lt] + 2 * i
    second = jnp.where(2 * i + 1 < meta[lt], first + 1, EMPTY)
    return (block(meta, lt, 2 * i), block(meta, lt, 2 * i + 1)), (first, second)


def both_bias(bias_ref, places):
    bias = tall(bias_ref[places[0]], bias_ref[places[1]]).astype(f32)
    return wide(bias, bias)


def run(turns, step, state):
    state = lax.fori_loop(0, turns // 2, lambda j, held: step(2 * j + 1, step(2 * j, held)), state)
    return lax.fori_loop(0, turns % 2, lambda _, held: step(turns - 1, held), state)


def turn_blocks(pairs, turned_ref, ref):
    def turn(i, _):
        for j in range(4):
            for member in range(2):
                for pp in range(pairs):
                    chip = 4 * i + j
                    turned_ref[chip, member, cols(pp), :] = ref[chip, member, :, cols(pp)].T
        return 0

    lax.fori_loop(0, CHIPS // 4, turn, 0)


def rows_of(ref, blocks, pp):
    (c0, m0), (c1, m1) = blocks
    return tall(ref[c0, m0, :, cols(pp)], ref[c1, m1, :, cols(pp)])


def turned_of(ref, blocks, pp):
    (c0, m0), (c1, m1) = blocks
    return wide(ref[c0, m0, cols(pp), :], ref[c1, m1, cols(pp), :])


def add_rows(ref, blocks, kind, pp, part):
    for (chip, member), rows in zip(blocks, (part[:BLK], part[BLK:])):
        ref[kind, chip, member, :, cols(pp)] += rows


def fetch(copies, sem):
    copies = [
        pltpu.make_async_copy(source, target, sem.at[i]) for i, (source, target) in enumerate(copies)
    ]
    for copy in copies:
        copy.start()

    def wait():
        for copy in copies:
            copy.wait()

    return wait


def forward_kernel(
    pairs, meta, qg_ref, value_ref, kv_hbm, bias_hbm, acc_ref, stat_ref,
    vt_ref, query_ref, score_ref, key_ref, bias_ref, sem,
):
    wait = fetch([(kv_hbm.at[:, 0], key_ref), (bias_hbm, bias_ref)], sem)
    turn_blocks(pairs, vt_ref, value_ref)
    for lt in range(NT):
        for pp in range(pairs):
            query_ref[lt, pp] = split_cols(qg_ref[lt, 0, :, cols(pp)])
    wait()

    def target(lt, _):
        turns = (meta[lt] + 1) // 2

        def score_step(i, tops):
            blocks, places = tiles(meta, lt, i)
            bias = both_bias(bias_ref, places)
            out = []
            for pp in range(pairs):
                keys = rows_of(key_ref, blocks, pp)
                scores = dot(keys, query_ref[lt, pp]) * BASE2 + bias
                score_ref[i, pp] = scores
                top = jnp.max(scores.reshape(-1, 8, 2 * BLK), axis=0)
                out.append(jnp.maximum(tops[pp], top))
            return tuple(out)

        tops = run(turns, score_step, tuple(jnp.full((8, 2 * BLK), LOW, f32) for _ in range(pairs)))
        tops = [jnp.max(top, axis=0, keepdims=True) for top in tops]

        def weight_step(i, state):
            blocks, _ = tiles(meta, lt, i)
            out = []
            for pp in range(pairs):
                total, acc = state[pp]
                weights = jnp.exp2(score_ref[i, pp] - tops[pp])
                total = total + jnp.sum(weights.reshape(-1, 8, 2 * BLK), axis=0)
                low = weights.astype(bf16)
                vt = turned_of(vt_ref, blocks, pp)
                part = wide(dot(vt[:HEAD], low[:, :BLK]), dot(vt[HEAD:], low[:, BLK:]))
                out.append((total, acc + part))
            return tuple(out)

        start = tuple(
            (jnp.zeros((8, 2 * BLK), f32), jnp.zeros((HEAD, 2 * BLK), f32)) for _ in range(pairs)
        )
        state = run(turns, weight_step, start)
        for pp in range(pairs):
            total, acc = state[pp]
            acc_ref[lt, pp] = acc
            stat_ref[pp, pl.ds(lt, 1), :] = tops[pp]
            stat_ref[pp, pl.ds(NT + lt, 1), :] = jnp.sum(total, axis=0, keepdims=True)
        return 0

    lax.fori_loop(0, NT, target, 0)
    for pp in range(pairs):
        deltas = []
        for lt in range(NT):
            grad = qg_ref[lt, 1, :, cols(pp)].T.astype(f32)
            grad = wide(grad[:HEAD], grad[HEAD:])
            deltas.append(jnp.sum(acc_ref[lt, pp] * grad, axis=0, keepdims=True))
        stat_ref[pp, 2 * NT :, :] = jnp.concatenate(deltas)


def spec(shape, *index):
    return pl.BlockSpec(shape, lambda p, s: index, pipeline_mode=pl.Buffered(1))


HBM = pl.BlockSpec(memory_space=pl.ANY)


def specs(pairs, start):
    width = pairs * BLK
    return (
        spec((NT, 2, BLK, width), 0, 0, 0, start // pairs),
        [spec((CHIPS, None, 2, BLK, width), 0, kind, 0, 0, 0) for kind in range(2)],
        spec((NT, pairs, HEAD, 2 * BLK), 0, 0, 0, 0),
        spec((pairs, 3 * NT, 2 * BLK), 0, 0, 0),
    )


def forward(meta, pairs, start, qg, kv, bias):
    qg_spec, kv_specs, acc_spec, stat_spec = specs(pairs, start)
    return pl.pallas_call(
        functools.partial(forward_kernel, pairs),
        grid_spec=pltpu.PrefetchScalarGridSpec(
            num_scalar_prefetch=1,
            grid=(1,),
            in_specs=[qg_spec, kv_specs[1]] + [HBM] * 2,
            out_specs=[acc_spec, stat_spec],
            scratch_shapes=[
                pltpu.VMEM((CHIPS, 2, pairs * BLK, BLK), bf16),
                pltpu.VMEM((NT, pairs, BLK, 2 * BLK), bf16),
                pltpu.VMEM((NS // 2, pairs, 2 * BLK, 2 * BLK), f32),
                pltpu.VMEM((CHIPS, 2, BLK, pairs * BLK), bf16),
                pltpu.VMEM((EMPTY + 1, BLK, BLK), bf16),
                pltpu.SemaphoreType.DMA((2,)),
            ],
        ),
        out_shape=[
            jax.ShapeDtypeStruct((NT, pairs, HEAD, 2 * BLK), f32),
            jax.ShapeDtypeStruct((pairs, 3 * NT, 2 * BLK), f32),
        ],
        compiler_params=pltpu.CompilerParams(vmem_limit_bytes=VMEM),
        cost_estimate=pl.CostEstimate(
            flops=10**10, bytes_accessed=20 * 2**20, transcendentals=10**7
        ),
        name="forward" + str(start),
    )(meta, qg, kv, kv, bias)


def backward_kernel(
    pairs, meta, qg_ref, key_ref, kv_hbm, bias_hbm, acc_hbm, own_ref, one_ref, two_ref, three_ref,
    dkv_ref, dqa_ref, kt_ref, turned_ref, dq_ref, sum_ref, row_ref, value_ref, bias_ref, acc_ref, sem,
):
    copies = [(kv_hbm.at[:, 1], value_ref), (bias_hbm, bias_ref), (acc_hbm, acc_ref)]
    wait = fetch(copies, sem)
    turn_blocks(pairs, kt_ref, key_ref)
    for lt in range(NT):
        for pp in range(pairs):
            for kind in range(2):
                turned_ref[lt, pp, kind] = split_cols(qg_ref[lt, kind, :, cols(pp)])
    sum_ref[...] = jnp.zeros_like(sum_ref)
    for pp in range(pairs):
        parts = []
        for back, ref in enumerate((own_ref, one_ref, two_ref, three_ref)):
            stat = [ref[pp, part * NT : (part + 1) * NT, :] for part in range(3)]
            if back:
                stat = [pltpu.roll(rows, 2 * back, 0) for rows in stat]
            parts.append(stat)
        top = jnp.maximum(
            jnp.maximum(parts[0][0], parts[1][0]), jnp.maximum(parts[2][0], parts[3][0])
        )
        factors = [jnp.exp2(stat[0] - top) for stat in parts]
        total = sum(stat[1] * factor for stat, factor in zip(parts, factors))
        delta = sum(stat[2] * factor for stat, factor in zip(parts, factors))
        log_total = top + jnp.log2(total)
        row_ref[pp, :NT, :] = log_total
        row_ref[pp, NT : 2 * NT, :] = delta / total
        row_ref[pp, 2 * NT :, :] = jnp.exp2(parts[0][0] - log_total)
    wait()

    def target(lt, _):
        rows = [
            [split_rows(qg_ref[lt, kind, :, cols(pp)]) for kind in range(2)] for pp in range(pairs)
        ]
        log_totals = [row_ref[pp, pl.ds(lt, 1), :] for pp in range(pairs)]
        deltas = [row_ref[pp, pl.ds(NT + lt, 1), :] for pp in range(pairs)]

        def step(i, state):
            blocks, places = tiles(meta, lt, i)
            bias = both_bias(bias_ref, places)
            out = []
            for pp in range(pairs):
                keys = rows_of(key_ref, blocks, pp)
                values = rows_of(value_ref, blocks, pp)
                scores = dot(keys, turned_ref[lt, pp, 0]) * BASE2 + bias
                probs = jnp.exp2(scores - log_totals[pp])
                grad_prob = dot(values, turned_ref[lt, pp, 1])
                grad_score = (probs * (grad_prob - deltas[pp])).astype(bf16)
                value_part = dot(probs.astype(bf16), rows[pp][1])
                key_part = dot(grad_score, rows[pp][0])
                add_rows(sum_ref, blocks, 0, pp, key_part)
                add_rows(sum_ref, blocks, 1, pp, value_part)
                kt = turned_of(kt_ref, blocks, pp)
                part = wide(
                    dot(kt[:HEAD], grad_score[:, :BLK]), dot(kt[HEAD:], grad_score[:, BLK:])
                )
                out.append(state[pp] + part)
            return tuple(out)

        start = tuple(jnp.zeros((HEAD, 2 * BLK), f32) for _ in range(pairs))
        state = run((meta[lt] + 1) // 2, step, start)
        for pp in range(pairs):
            dq_ref[lt, pp] = state[pp] * SCALE
        return 0

    lax.fori_loop(0, NT, target, 0)

    def finish(i, _):
        for lt in (2 * i, 2 * i + 1):
            for pp in range(pairs):
                attended = acc_ref[lt, pp] * row_ref[pp, pl.ds(2 * NT + lt, 1), :]
                for kind, pair in enumerate((attended, dq_ref[lt, pp])):
                    pair = tall(pair[:, :BLK], pair[:, BLK:])
                    dqa_ref[lt, kind, :, cols(pp)] = pair.T.astype(bf16)
        return 0

    lax.fori_loop(0, NT // 2, finish, 0)
    dkv_ref[:, :, 0] = (sum_ref[0] * SCALE).astype(bf16)
    dkv_ref[:, :, 1] = sum_ref[1].astype(bf16)


def backward(meta, pairs, start, qg, kv, bias, acc, stats):
    qg_spec, kv_specs, acc_spec, stat_spec = specs(pairs, start)
    width = pairs * BLK
    return pl.pallas_call(
        functools.partial(backward_kernel, pairs),
        grid_spec=pltpu.PrefetchScalarGridSpec(
            num_scalar_prefetch=1,
            grid=(1,),
            in_specs=[qg_spec, kv_specs[0]] + [HBM] * 3 + [stat_spec] * 4,
            out_specs=[
                spec((CHIPS, 2, 2, BLK, width), 0, 0, 0, 0, 0),
                spec((NT, 2, BLK, width), 0, 0, 0, 0),
            ],
            scratch_shapes=[
                pltpu.VMEM((CHIPS, 2, width, BLK), bf16),
                pltpu.VMEM((NT, pairs, 2, BLK, 2 * BLK), bf16),
                pltpu.VMEM((NT, pairs, HEAD, 2 * BLK), f32),
                pltpu.VMEM((2, CHIPS, 2, BLK, width), f32),
                pltpu.VMEM((pairs, 3 * NT, 2 * BLK), f32),
                pltpu.VMEM((CHIPS, 2, BLK, width), bf16),
                pltpu.VMEM((EMPTY + 1, BLK, BLK), bf16),
                pltpu.VMEM((NT, pairs, HEAD, 2 * BLK), f32),
                pltpu.SemaphoreType.DMA((3,)),
            ],
        ),
        out_shape=[
            jax.ShapeDtypeStruct((CHIPS, 2, 2, BLK, width), bf16),
            jax.ShapeDtypeStruct((NT, 2, BLK, width), bf16),
        ],
        compiler_params=pltpu.CompilerParams(vmem_limit_bytes=VMEM),
        cost_estimate=pl.CostEstimate(
            flops=2 * 10**10, bytes_accessed=30 * 2**20, transcendentals=10**7
        ),
        name="backward" + str(start),
    )(meta, qg, kv, kv, bias, acc, *stats)


def steps_back(rows, z):
    turned = jnp.concatenate([rows[:1], rows[3:], rows[2:3], rows[1:2]])
    return lax.dynamic_slice_in_dim(jnp.concatenate([turned, turned]), 4 - z, 4)


def tile_lists(own_adj, got_adj, side, z):
    adj = jnp.stack([own_adj, got_adj], axis=1)
    count = jnp.sum(adj, axis=2)
    first = jnp.cumsum(count, axis=0) - count + jnp.array([0, MAXT])
    adj = steps_back(adj, z).reshape(NT, NS)
    count = steps_back(count, z).reshape(NT)
    first = steps_back(first, z).reshape(NT)
    place = jnp.cumsum(adj, axis=1) - 1
    hit = (adj[:, None, :] > 0) & (place[:, None, :] == jnp.arange(NS)[None, :, None])
    held = jnp.arange(NS) ^ side
    source = jnp.sum(jnp.where(hit, held[None, None, :], 0), axis=2)
    return jnp.concatenate([count, first, source.reshape(-1)]).astype(jnp.int32)


SWAP = [(0, 1), (1, 0)]


def back(array, steps, axis="z"):
    return lax.ppermute(array, axis, [(s, (s + steps) % 4) for s in range(4)])


def half(array, side):
    return lax.dynamic_slice_in_dim(array, side * HALF, HALF, array.ndim - 1)


def chip_pair(first, second, side, axis):
    both = jnp.stack([first, second])
    got = lax.ppermute(half(both, 1 - side), "k", SWAP)
    return jnp.stack([half(both, side), got], axis=axis)


def ring_reduce(parts, axis):
    here = lax.axis_index(axis)
    own, right, far, left = (
        lax.dynamic_index_in_dim(parts, (here + steps) % 4, 0, False) for steps in range(4)
    )
    middle = far.shape[0] // 2
    onward = back(far[:middle], 1, axis)
    backward_half = back(far[middle:], -1, axis)

    def add(mine, got):
        return (mine.astype(f32) + got.astype(f32)).astype(bf16)

    right = jnp.concatenate([add(right[:middle], onward), right[middle:]])
    left = jnp.concatenate([left[:middle], add(left[middle:], backward_half)])
    right, left = back(right, 1, axis), back(left, -1, axis)
    return own.astype(f32) + right.astype(f32) + left.astype(f32)


def plane_sum(parts):
    rows = ring_reduce(parts.reshape(4, 4 * 4 * BLK, -1), "y").astype(bf16)
    return ring_reduce(rows.reshape(4, 4 * BLK, -1), "x").astype(bf16)


def own_blocks(part, side):
    got = lax.ppermute(part[1], "k", SWAP)
    whole = jnp.where(
        side == 0,
        jnp.concatenate([part[0], got], axis=-1),
        jnp.concatenate([got, part[0]], axis=-1),
    )
    return whole[0], whole[1]


def z_sum(part):
    part = part.reshape(4, 2, 2, BLK, -1)
    total = part[0].astype(f32)
    for steps in (1, 2, 3):
        total = total + back(part[steps], -steps).astype(f32)
    return total.astype(bf16)


def shards(node_query, node_key, node_value, grad_out, block_adjacency, edge_mask):
    side, z = lax.axis_index("k"), lax.axis_index("z")
    plane = ("y", "x")
    kv = chip_pair(node_key, node_value, side, 1)
    groups, start = [], 0
    for pairs in GROUPS:
        width = pairs * BLK
        part = kv[..., start * BLK : start * BLK + width].reshape(4 * BLK, width)
        whole = lax.all_gather(part, plane, axis=0, tiled=True)
        groups.append((pairs, start, whole.reshape(CHIPS, 2, 2, BLK, width)))
        start += pairs
    qg = chip_pair(node_query, grad_out, side, 0).reshape(4 * BLK, HALF)
    qg = jnp.concatenate([qg] + [back(qg, steps) for steps in (1, 2, 3)])
    qg = qg.reshape(NT, 2, BLK, HALF)
    own_adj = (block_adjacency > 0).astype(jnp.int32)
    own_bias = bias_tiles(own_adj, edge_mask)
    got_bias = lax.ppermute(own_bias, "k", SWAP)
    bias = jnp.concatenate([own_bias, got_bias, jnp.full((1, BLK, BLK), LOW, bf16)])
    got_adj = lax.ppermute(own_adj, "k", SWAP)
    meta = tile_lists(own_adj, got_adj, side, z)
    sources, targets = [], []
    for pairs, start, whole in groups:
        acc, own = forward(meta, pairs, start, qg, whole, bias)
        stats = [own] + [back(own, steps) for steps in (1, 2, 3)]
        dkv, dqa = backward(meta, pairs, start, qg, whole, bias, acc, stats)
        dkv = dkv.reshape(NS * 2 * BLK, pairs * BLK)
        if start == 0:
            dkv = lax.psum_scatter(dkv, plane, scatter_dimension=0, tiled=True)
        else:
            dkv, targets[0] = lax.optimization_barrier((dkv, targets[0]))
            dkv = plane_sum(dkv)
        sources.append(dkv.reshape(2, 2, BLK, -1))
        targets.append(z_sum(dqa))
    attended, grad_query = own_blocks(jnp.concatenate(targets, axis=-1), side)
    grad_key, grad_value = own_blocks(jnp.concatenate(sources, axis=-1), side)
    return (attended, grad_query, grad_key, grad_value)


def solution(mesh):
    fine = Mesh(mesh.devices.reshape(4, 4, 2, 4), ("y", "x", "k", "z"))
    row = ("y", "x", "k")
    target = P(row + ("z",), None)
    source = P(("z",) + row, None)
    tile = P(row, "z")
    return jax.shard_map(
        shards,
        mesh=fine,
        in_specs=(target, source, source, target, tile, tile),
        out_specs=(target, target, source, source),
        check_vma=False,
    )
```
